32 devices in a mesh: dp: 8 (over z, x), tensor: 4 (over y, core).
Axes of the slice: x: 2, y: 2, z: 4, core: 2. Of those that a mesh axis runs over, the one named last changes fastest.
Arguments:
- inputs: bfloat16 [8192, 768], P(('dp', 'tensor')), may hold values from -6 to 6
- cotangent: bfloat16 [8192, 768], P(('dp', 'tensor')), may hold values from -6 to 6
- qkv_weight: bfloat16 [3, 768, 768], P(None, 'dp', 'tensor'), may hold values from -0.21582031 to 0.21582031
- proj_weight: bfloat16 [768, 768], P('tensor', 'dp'), may hold values from -3.453125 to 3.453125
- up_weight: bfloat16 [768, 3072], P('dp', 'tensor'), may hold values from -0.21875 to 0.21875
- down_weight: bfloat16 [3072, 768], P('tensor', 'dp'), may hold values from -0.109375 to 0.109375
- qv_bias: bfloat16 [2, 768], P(None, ('tensor', 'dp')), may hold values from -3 to 3
- up_bias: bfloat16 [3072], P(('tensor', 'dp')), may hold values from -3 to 3
- norm_gains: bfloat16 [2, 768], P(None, ('dp', 'tensor')), may hold values from 0.5 to 1.5
- row_biases: bfloat16 [4, 768], P(None, ('dp', 'tensor')), may hold values from -3 to 3
Outputs:
- outputs: bfloat16 [8192, 768], P(('dp', 'tensor'))
- input_grad: float32 [8192, 768], P(('dp', 'tensor'))
- qkv_grad: float32 [3, 768, 768], P(None, 'dp', 'tensor')
- proj_grad: float32 [768, 768], P('tensor', 'dp')
- up_grad: float32 [768, 3072], P('dp', 'tensor')
- down_grad: float32 [3072, 768], P('tensor', 'dp')
- qv_bias_grad: float32 [2, 768], P(None, ('tensor', 'dp'))
- up_bias_grad: float32 [3072], P(('tensor', 'dp'))
- gains_grad: float32 [2, 768], P(None, ('dp', 'tensor'))
- biases_grad: float32 [4, 768], P(None, ('dp', 'tensor'))
The draws below stay inside these ranges and needn't reach their ends.
All inputs are finite; a program needn't handle non-finite values.
Results may differ from the reference program's by a relative error of at most 0.018.
The reference program's roundings to bfloat16 on the way count: a program that leaves them out, or rounds other values in their place, can miss the bound.
Values may be sent and summed in bfloat16 or wider, within the bound.
A program may use at most 128 MiB of HBM per device.

```python
import jax
import jax.numpy as jnp
from jax import lax

D = 768
H = 12
HD = 64
FF = 3072
FRAMES = 1024
CLIPS = 8


def block_levels(key, dims, cuts, least, largest):
    factor_of, own = 1.0, jax.random.fold_in(key, 6)
    for position, parts in cuts:
        draws = jnp.exp(jax.random.uniform(jax.random.fold_in(own, position), (parts,), jnp.float32, least / len(cuts), largest / len(cuts)))
        factor_of = factor_of * jnp.repeat(draws, dims[position] // parts).reshape([-1 if axis == position else 1 for axis in range(len(dims))])
    return factor_of


def noise(stream_key, extent, deviation, reach, shards=(), held_as=jnp.bfloat16):
    factor_of = block_levels(stream_key, extent, shards, -0.22, 0.18) if shards else 1.0
    entries = jax.random.normal(stream_key, extent, jnp.float32) * deviation * factor_of
    return jnp.minimum(jnp.maximum(entries, -reach), reach).astype(held_as)


def setup_inputs(seed: int = 0) -> dict:
    key_list = jax.random.split(jax.random.key(seed), 11)
    return {
        "inputs": noise(key_list[0], (CLIPS * FRAMES, D), 1.0, 6.0, ((0, 32),)),
        "cotangent": noise(key_list[1], (CLIPS * FRAMES, D), 1.0, 6.0, ((0, 32),)),
        "qkv_weight": noise(key_list[2], (3, D, D), (1.25 * D ** -0.5), 0.21582031, ((1, 8), (2, 4))),
        "proj_weight": noise(key_list[3], (D, D), (0.5 * (FRAMES * D ** -1) ** 0.5), 3.453125, ((0, 4), (1, 8))),
        "up_weight": noise(key_list[4], (D, FF), D ** -0.5, 0.21875, ((0, 8), (1, 4))),
        "down_weight": noise(key_list[5], (FF, D), FF ** -0.5, 0.109375, ((0, 4), (1, 8))),
        "qv_bias": noise(key_list[6], (2, D), 0.5, 3.0, ((1, 32),)),
        "up_bias": noise(key_list[7], (FF,), 0.5, 3.0, ((0, 32),)),
        "norm_gains": jnp.clip(1.0 + 0.1 * jax.random.normal(key_list[8], (2, D), jnp.float32), 0.5, 1.5).astype(jnp.bfloat16),
        "row_biases": noise(key_list[9], (4, D), 0.5, 3.0, ((1, 32),)),
    }


@jax.custom_vjp
def low(v):
    return lax.optimization_barrier(v.astype(jnp.bfloat16)).astype(jnp.float32)

@jax.custom_vjp
def low_back(v):
    return v

def low_keep(v):
    return (low(v), None)

def low_pass(kept, grad):
    return (grad,)

def back_keep(v):
    return (v, None)

def back_low(kept, grad):
    return (low(grad),)
low.defvjp(low_keep, low_pass)
low_back.defvjp(back_keep, back_low)
EPSILON = 1e-05
SCALE = 0.125
ROOT_HALF = 0.7071067811865476
HIGHEST = lax.Precision.HIGHEST

def layer_norm(values, gain_row, shift_row):
    center = values - lax.optimization_barrier(jnp.mean(values, axis=-1, keepdims=True))
    spread = lax.optimization_barrier(jnp.mean(center * center, axis=-1, keepdims=True))
    return center * lax.rsqrt(spread + EPSILON) * gain_row + shift_row

def gelu_exact(values):
    return 0.5 * values * (1.0 + jax.scipy.special.erf(values * ROOT_HALF))

def encoder_layer(clip_rows, params):
    qkv_weight, proj_weight, up_weight, down_weight, qv_bias, up_bias, norm_gains, row_biases = params
    normed = low(layer_norm(clip_rows, norm_gains[0], row_biases[0]))
    projected = jnp.einsum('td,cde->cte', normed, qkv_weight, precision=HIGHEST)
    queries = low(low_back(projected[0] + qv_bias[0])).reshape(FRAMES, H, HD)
    key_rows = low(low_back(projected[1])).reshape(FRAMES, H, HD)
    value_rows = low(low_back(projected[2] + qv_bias[1])).reshape(FRAMES, H, HD)
    scores = low_back(jnp.einsum('qhe,khe->hqk', queries, key_rows, precision=HIGHEST) * SCALE)
    row_max = lax.optimization_barrier(jnp.max(scores, axis=2, keepdims=True))
    exponent = jnp.exp(scores - row_max)
    attn_probs = exponent / lax.optimization_barrier(jnp.sum(exponent, axis=2, keepdims=True))
    mixture = jnp.einsum('hqk,khe->qhe', low(attn_probs), value_rows, precision=HIGHEST).reshape(FRAMES, D)
    attended = low(low_back(mixture))
    branch = low_back(jnp.dot(attended, proj_weight, precision=HIGHEST))
    middle = clip_rows + branch + row_biases[1]
    normed_two = low(layer_norm(middle, norm_gains[1], row_biases[2]))
    hidden = low_back(jnp.dot(normed_two, up_weight, precision=HIGHEST) + up_bias)
    activated = low(gelu_exact(hidden))
    feed_sum = low_back(jnp.dot(activated, down_weight, precision=HIGHEST))
    return middle + feed_sum + row_biases[3]

def reference(inputs, cotangent, qkv_weight, proj_weight, up_weight, down_weight, qv_bias, up_bias, norm_gains, row_biases):
    params = tuple((array.astype(jnp.float32) for array in (qkv_weight, proj_weight, up_weight, down_weight, qv_bias, up_bias, norm_gains, row_biases)))
    clips = inputs.astype(jnp.float32).reshape(CLIPS, FRAMES, D)
    seeds = cotangent.astype(jnp.float32).reshape(CLIPS, FRAMES, D)

    def advance(totals, paired):
        clip_rows, seed_rows = paired
        result, pullback = jax.vjp(encoder_layer, clip_rows, params)
        clip_grad, param_grads = pullback(seed_rows)
        totals = tuple((first + second for first, second in zip(totals, param_grads)))
        return (totals, (result.astype(jnp.bfloat16), clip_grad))
    initial = tuple((jnp.zeros_like(array) for array in params))
    totals, (results, clip_grads) = lax.scan(advance, initial, (clips, seeds))
    return (results.reshape(CLIPS * FRAMES, D), clip_grads.reshape(CLIPS * FRAMES, D), totals[0], totals[1], totals[2], totals[3], totals[4], totals[5], totals[6], totals[7])
```

```python
import functools

import jax
import jax.numpy as jnp
from jax import lax
from jax.experimental import pallas as pl
from jax.experimental.pallas import tpu as pltpu
from jax.sharding import PartitionSpec as P

HD = 64
EPSILON = 1e-05
SCALE = 0.125
ROOT_HALF = 0.7071067811865476
ROOT_TWO_PI_INVERSE = 0.3989422804014327
F32 = jnp.float32
BF16 = jnp.bfloat16
VMEM_LIMIT = 50 * 1024 * 1024
MESH = pl.DeviceIdType.MESH
TENSOR = 4


def layer_norm(values, gain_row, shift_row):
    center = values - jnp.mean(values, axis=-1, keepdims=True)
    spread = jnp.mean(center * center, axis=-1, keepdims=True)
    return center * lax.rsqrt(spread + EPSILON) * gain_row + shift_row


def norm_back(values, gain_row, incoming):
    center = values - jnp.mean(values, axis=-1, keepdims=True)
    spread = jnp.mean(center * center, axis=-1, keepdims=True)
    inverse = lax.rsqrt(spread + EPSILON)
    unit_rows = center * inverse
    scaled = incoming * gain_row
    grad_in = inverse * (
        scaled
        - jnp.mean(scaled, axis=-1, keepdims=True)
        - unit_rows * jnp.mean(scaled * unit_rows, axis=-1, keepdims=True)
    )
    return (
        grad_in,
        jnp.sum(incoming * unit_rows, axis=0, keepdims=True),
        jnp.sum(incoming, axis=0, keepdims=True),
    )


class Place:
    def __init__(self, dp):
        self.dp = dp
        self.zs = dp // 2
        self.d = lax.axis_index("dp")
        self.t = lax.axis_index("tensor")
        self.z = self.d // 2
        self.x = lax.rem(self.d, 2)
        self.core = self.t + 1 - 2 * lax.rem(self.t, 2)
        self.across = lax.rem(self.t + 2, TENSOR)
        self.diagonal = lax.rem(self.core + 2, TENSOR)

    def tensor_id(self, t):
        return {"dp": self.d, "tensor": t}

    def dp_id(self, d):
        return {"dp": d, "tensor": self.t}

    def x_id(self):
        return self.dp_id(self.z * 2 + 1 - self.x)

    def z_of(self, k):
        return lax.rem(self.z + k, self.zs)

    def z_from(self, k):
        return lax.rem(self.z + self.zs - k, self.zs)

    def z_id(self, k):
        return self.dp_id(self.z_of(k) * 2 + self.x)


def greet(peers):
    barrier = pltpu.get_barrier_semaphore()
    for peer in peers:
        pl.semaphore_signal(barrier, inc=1, device_id=peer, device_id_type=MESH)
    pl.semaphore_wait(barrier, len(peers))


def remote(src, dst, send, recv, peer):
    return pltpu.make_async_remote_copy(
        src_ref=src, dst_ref=dst, send_sem=send, recv_sem=recv, device_id=peer, device_id_type=MESH
    )


class TensorGather:
    def __init__(self, here, own, out, send, recv):
        t = here.t
        self.first = [
            remote(own, out.at[t], send.at[0], recv.at[0], here.tensor_id(here.across)),
            remote(own, out.at[t], send.at[1], recv.at[1], here.tensor_id(here.core)),
        ]
        landed = out.at[here.across]
        self.relay = remote(landed, landed, send.at[2], recv.at[2], here.tensor_id(here.core))

    def start(self):
        for copy in self.first:
            copy.start()

    def pass_on(self):
        self.first[0].wait_recv()
        self.relay.start()

    def finish(self):
        self.first[1].wait_recv()
        self.relay.wait_recv()
        self.first[0].wait_send()
        self.first[1].wait_send()
        self.relay.wait_send()


class TensorScatter:
    def __init__(self, here, part, from_core, to_across, from_across, send, recv):
        self.here, self.part = here, part
        self.from_core, self.to_across, self.from_across = from_core, to_across, from_across
        core = here.tensor_id(here.core)
        self.far = remote(part.at[here.diagonal], from_core.at[0], send.at[0], recv.at[0], core)
        self.near = remote(part.at[here.core], from_core.at[1], send.at[1], recv.at[1], core)
        self.cross = remote(
            to_across, from_across, send.at[2], recv.at[2], here.tensor_id(here.across)
        )

    def start(self):
        self.far.start()
        self.near.start()

    def pass_on(self):
        self.far.wait_recv()
        total = self.part[self.here.across].astype(F32) + self.from_core[0].astype(F32)
        self.to_across[...] = total.astype(BF16)
        self.cross.start()

    def result(self):
        self.near.wait_recv()
        total = self.part[self.here.t].astype(F32) + self.from_core[1].astype(F32)
        self.cross.wait_recv()
        return total + self.from_across[...].astype(F32)

    def finish(self):
        self.far.wait_send()
        self.near.wait_send()
        self.cross.wait_send()


def scatter_scratch(rows, width):
    return [
        pltpu.VMEM((2, rows, width), BF16),
        pltpu.VMEM((rows, width), BF16),
        pltpu.VMEM((rows, width), BF16),
        pltpu.SemaphoreType.DMA((3,)),
        pltpu.SemaphoreType.DMA((3,)),
    ]


class WeightGather:
    def __init__(self, here, own, out, sz, rz, sx, rx, local):
        self.zs = here.zs
        mine = out.at[here.z, here.x]
        self.keep = pltpu.make_async_copy(own, mine, local)
        self.along = [None] + [
            remote(own, mine, sz.at[k], rz.at[k], here.z_id(k)) for k in range(1, self.zs)
        ]
        self.over = [remote(own, mine, sx.at[0], rx.at[0], here.x_id())]
        for k in range(1, self.zs):
            landed = out.at[here.z_from(k), here.x]
            self.over.append(remote(landed, landed, sx.at[k], rx.at[k], here.x_id()))

    def start(self):
        for copy in self.along[1:]:
            copy.start()
        self.over[0].start()
        self.keep.start()

    def pass_on(self, k):
        self.along[k].wait_recv()
        self.over[k].start()

    def finish(self):
        for copy in self.over:
            copy.wait_recv()
        for copy in self.along[1:] + self.over:
            copy.wait_send()
        self.keep.wait()


def weight_sems(zs):
    return [pltpu.SemaphoreType.DMA((zs,))] * 4 + [pltpu.SemaphoreType.DMA]


class GradScatter:
    def __init__(self, here, part, from_x, to_z, from_z, sz, rz, sx, rx):
        self.here, self.part = here, part
        self.from_x, self.to_z, self.from_z = from_x, to_z, from_z
        self.order = list(range(1, here.zs)) + [0]
        self.over, self.along = {}, {}
        for k in self.order:
            slot = here.z_of(k)
            self.over[k] = remote(
                part.at[slot, 1 - here.x], from_x.at[k], sx.at[k], rx.at[k], here.x_id()
            )
            if k:
                self.along[k] = remote(to_z.at[k], from_z.at[k], sz.at[k], rz.at[k], here.z_id(k))

    def start(self):
        for k in self.order:
            self.over[k].start()

    def half(self, k):
        here = self.here
        self.over[k].wait_recv()
        return self.part[here.z_of(k), here.x].astype(F32) + self.from_x[k].astype(F32)

    def pass_on(self, k):
        self.to_z[k] = self.half(k).astype(BF16)
        self.along[k].start()

    def result(self):
        total = self.half(0)
        for k in range(1, self.here.zs):
            self.along[k].wait_recv()
            total = total + self.from_z[k].astype(F32)
        return total

    def finish(self):
        for k in self.order:
            self.over[k].wait_send()
            if k:
                self.along[k].wait_send()


def grad_scratch(zs, rows, width):
    return [pltpu.VMEM((zs, rows, width), BF16)] * 3 + [pltpu.SemaphoreType.DMA((zs,))] * 4


def tensor_peers(here):
    return [here.tensor_id(t) for t in (here.core, here.across, here.diagonal)]


def dp_peers(here):
    return [here.dp_id(lax.rem(here.d + k, here.dp)) for k in range(1, here.dp)]


def gather_kernel(dp, x_ref, c_ref, wa_ref, wb_ref, s_ref, x_out, c_out, wa_out, wb_out, s_out, *sems):
    here = Place(dp)
    gx = sems[0:2]
    gc = sems[2:4]
    wa = sems[4:9]
    wb = sems[9:14]
    st_send, st_recv, sd_send, sd_recv, local = sems[14:19]
    greet(tensor_peers(here) + dp_peers(here))
    keeps = [
        pltpu.make_async_copy(x_ref, x_out.at[here.t], local.at[0]),
        pltpu.make_async_copy(c_ref, c_out.at[here.t], local.at[1]),
        pltpu.make_async_copy(s_ref, s_out.at[here.d, here.t], local.at[2]),
    ]
    for copy in keeps:
        copy.start()
    small = [
        remote(s_ref, s_out.at[here.d, here.t], st_send.at[i], st_recv.at[i], peer)
        for i, peer in enumerate(tensor_peers(here))
    ]
    for copy in small:
        copy.start()
    x_gather = TensorGather(here, x_ref, x_out, *gx)
    x_gather.start()
    a_gather = WeightGather(here, wa_ref, wa_out, *wa)
    a_gather.start()
    for copy in small:
        copy.wait_recv()
    keeps[2].wait()
    row = s_out.at[here.d]
    spread = [
        remote(row, row, sd_send.at[k], sd_recv.at[k], here.dp_id(lax.rem(here.d + k, dp)))
        for k in range(1, dp)
    ]
    for copy in spread:
        copy.start()
    b_gather = WeightGather(here, wb_ref, wb_out, *wb)
    b_gather.start()
    c_gather = TensorGather(here, c_ref, c_out, *gc)
    c_gather.start()
    x_gather.pass_on()
    for k in range(1, here.zs):
        a_gather.pass_on(k)
    c_gather.pass_on()
    for k in range(1, here.zs):
        b_gather.pass_on(k)
    x_gather.finish()
    c_gather.finish()
    a_gather.finish()
    b_gather.finish()
    for copy in spread:
        copy.wait_recv()
    for copy in small + spread:
        copy.wait_send()
    keeps[0].wait()
    keeps[1].wait()


def gather_all(dp, x, cot, wa, wb, small):
    zs = dp // 2
    anywhere = pl.BlockSpec(memory_space=pl.ANY)
    dma = pltpu.SemaphoreType.DMA
    shape = jax.ShapeDtypeStruct
    return pl.pallas_call(
        functools.partial(gather_kernel, dp),
        out_shape=(
            shape((TENSOR,) + x.shape, BF16),
            shape((TENSOR,) + x.shape, BF16),
            shape((zs, 2) + wa.shape, BF16),
            shape((zs, 2) + wb.shape, BF16),
            shape((dp, TENSOR) + small.shape, BF16),
        ),
        in_specs=[anywhere] * 5,
        out_specs=(anywhere,) * 5,
        scratch_shapes=[dma((3,))] * 4
        + weight_sems(zs) * 2
        + [dma((3,)), dma((3,)), dma((dp,)), dma((dp,)), dma((3,))],
        compiler_params=pltpu.CompilerParams(
            collective_id=0, has_side_effects=True, vmem_limit_bytes=VMEM_LIMIT
        ),
    )(x, cot, wa, wb, small)


def middle_kernel(dp, part, x_ref, vec, middle_out, two_out, *rest):
    here = Place(dp)
    scatter = TensorScatter(here, part, *rest[0:5])
    gather = TensorGather(here, two_out.at[here.t], two_out, *rest[5:7])
    greet(tensor_peers(here))
    scatter.start()
    scatter.pass_on()
    middle = x_ref[...].astype(F32) + scatter.result() + vec[3:4]
    middle_out[...] = middle
    two_out[here.t] = layer_norm(middle, vec[1:2], vec[4:5]).astype(BF16)
    gather.start()
    gather.pass_on()
    gather.finish()
    scatter.finish()


def make_middle(dp, part, x, vec):
    vmem = pl.BlockSpec(memory_space=pltpu.VMEM)
    rows, width = x.shape
    dma = pltpu.SemaphoreType.DMA
    return pl.pallas_call(
        functools.partial(middle_kernel, dp),
        out_shape=(
            jax.ShapeDtypeStruct((rows, width), F32),
            jax.ShapeDtypeStruct((TENSOR, rows, width), BF16),
        ),
        in_specs=[vmem] * 3,
        out_specs=(vmem,) * 2,
        scratch_shapes=scatter_scratch(rows, width) + [dma((3,)), dma((3,))],
        compiler_params=pltpu.CompilerParams(
            collective_id=1, has_side_effects=True, vmem_limit_bytes=VMEM_LIMIT
        ),
    )(part, x, vec)


def back_kernel(dp, grad_part, feed_part, middle, cot, vec, out, mgrad_out, attn_out, sums, *rest):
    here = Place(dp)
    grad_scatter = TensorScatter(here, grad_part, *rest[0:5])
    feed_scatter = TensorScatter(here, feed_part, *rest[5:10])
    gather = TensorGather(here, attn_out.at[here.t], attn_out, *rest[10:12])
    greet(tensor_peers(here))
    grad_scatter.start()
    feed_scatter.start()
    grad_scatter.pass_on()
    incoming = grad_scatter.result()
    mid = middle[...]
    part, gain_sum, shift_sum = norm_back(mid, vec[1:2], incoming)
    grad_out = cot[...].astype(F32)
    mgrad = grad_out + part
    attn_out[here.t] = mgrad.astype(BF16)
    gather.start()
    feed_scatter.pass_on()
    mgrad_out[...] = mgrad
    sums[0:1] = gain_sum
    sums[1:2] = jnp.sum(mgrad, axis=0, keepdims=True)
    sums[2:3] = shift_sum
    sums[3:4] = jnp.sum(grad_out, axis=0, keepdims=True)
    gather.pass_on()
    out[...] = (mid + feed_scatter.result() + vec[5:6]).astype(BF16)
    gather.finish()
    grad_scatter.finish()
    feed_scatter.finish()


def go_back(dp, grad_part, feed_part, middle, cot, vec):
    vmem = pl.BlockSpec(memory_space=pltpu.VMEM)
    rows, width = cot.shape
    dma = pltpu.SemaphoreType.DMA
    shape = jax.ShapeDtypeStruct
    return pl.pallas_call(
        functools.partial(back_kernel, dp),
        out_shape=(
            shape((rows, width), BF16),
            shape((rows, width), F32),
            shape((TENSOR, rows, width), BF16),
            shape((4, width), F32),
        ),
        in_specs=[vmem] * 5,
        out_specs=(vmem,) * 4,
        scratch_shapes=scatter_scratch(rows, width) * 2 + [dma((3,)), dma((3,))],
        compiler_params=pltpu.CompilerParams(
            collective_id=2, has_side_effects=True, vmem_limit_bytes=VMEM_LIMIT
        ),
    )(grad_part, feed_part, middle, cot, vec)


def last_kernel(
    dp, part, x_ref, mgrad, vec, sums, own_sums, ga, gb,
    in_out, ga_out, gb_out, sum_out, *rest
):
    here = Place(dp)
    scatter = TensorScatter(here, part, *rest[0:5])
    a_scatter = GradScatter(here, ga, *rest[5:12])
    b_scatter = GradScatter(here, gb, *rest[12:19])
    near, around, st_send, st_recv, sd_send, sd_recv = rest[19:25]
    greet(tensor_peers(here) + dp_peers(here))
    scatter.start()
    b_scatter.start()
    a_scatter.start()
    scatter.pass_on()
    x = x_ref[...].astype(F32)
    in_part, gain_sum, shift_sum = norm_back(x, vec[0:1], scatter.result())
    in_out[...] = mgrad[...] + in_part
    near[0, 0:1] = gain_sum
    near[0, 1:2] = sums[0:1]
    near[0, 2:3] = shift_sum
    near[0, 3:6] = sums[1:4]
    near[0, 6:8] = jnp.zeros_like(near[0, 6:8])
    small = [
        remote(near.at[0], near.at[i + 1], st_send.at[i], st_recv.at[i], peer)
        for i, peer in enumerate(tensor_peers(here))
    ]
    for copy in small:
        copy.start()
    for k in range(1, here.zs):
        b_scatter.pass_on(k)
    for copy in small:
        copy.wait_recv()
    around[0, 0:8] = (near[0] + near[1]) + (near[2] + near[3])
    around[0, 8:16] = own_sums[...]
    spread = [
        remote(
            around.at[0], around.at[k], sd_send.at[k], sd_recv.at[k],
            here.dp_id(lax.rem(here.d + k, dp)),
        )
        for k in range(1, dp)
    ]
    for copy in spread:
        copy.start()
    for k in range(1, here.zs):
        a_scatter.pass_on(k)
    gb_out[...] = b_scatter.result()
    total = around[0]
    for k in range(1, dp):
        spread[k - 1].wait_recv()
        total = total + around[k]
    sum_out[...] = total
    ga_out[...] = a_scatter.result()
    scatter.finish()
    a_scatter.finish()
    b_scatter.finish()
    for copy in small + spread:
        copy.wait_send()


def finish_all(dp, part, x, mgrad, vec, sums, own_sums, ga, gb):
    zs = dp // 2
    vmem = pl.BlockSpec(memory_space=pltpu.VMEM)
    rows, width = x.shape
    dma = pltpu.SemaphoreType.DMA
    shape = jax.ShapeDtypeStruct
    return pl.pallas_call(
        functools.partial(last_kernel, dp),
        out_shape=(
            shape((rows, width), F32),
            shape(ga.shape[2:], F32),
            shape(gb.shape[2:], F32),
            shape((16, width), F32),
        ),
        in_specs=[vmem] * 8,
        out_specs=(vmem,) * 4,
        scratch_shapes=scatter_scratch(rows, width)
        + grad_scratch(zs, *ga.shape[2:])
        + grad_scratch(zs, *gb.shape[2:])
        + [pltpu.VMEM((TENSOR, 8, width), F32), pltpu.VMEM((dp, 16, width), F32)]
        + [dma((3,)), dma((3,)), dma((dp,)), dma((dp,))],
        compiler_params=pltpu.CompilerParams(
            collective_id=3, has_side_effects=True, vmem_limit_bytes=VMEM_LIMIT
        ),
    )(part, x, mgrad, vec, sums, own_sums, ga, gb)


def attend_kernel(q_ref, k_ref, v_ref, out_ref, log_ref):
    scores = (
        lax.dot_general(q_ref[0], k_ref[0], (((1,), (1,)), ((), ())), preferred_element_type=F32)
        * SCALE
    )
    top = jnp.max(scores, axis=1, keepdims=True)
    exponent = jnp.exp(scores - top)
    total = jnp.sum(exponent, axis=1, keepdims=True)
    probs = (exponent * (1.0 / total)).astype(BF16)
    out_ref[0] = jnp.dot(probs, v_ref[0], preferred_element_type=F32).astype(BF16)
    log_ref[0] = top + jnp.log(total)


def attend(q, k, v, block):
    heads, frames, width = q.shape
    some = pl.BlockSpec((1, block, width), lambda h, i: (h, i, 0))
    every = pl.BlockSpec((1, frames, width), lambda h, i: (h, 0, 0))
    return pl.pallas_call(
        attend_kernel,
        grid=(heads, frames // block),
        out_shape=(
            jax.ShapeDtypeStruct(q.shape, BF16),
            jax.ShapeDtypeStruct((heads, frames, 1), F32),
        ),
        in_specs=[some, every, every],
        out_specs=(some, pl.BlockSpec((1, block, 1), lambda h, i: (h, i, 0))),
        compiler_params=pltpu.CompilerParams(vmem_limit_bytes=VMEM_LIMIT),
    )(q, k, v)


def attend_back_kernel(q_ref, g_ref, log_ref, k_ref, v_ref, dq_ref, dk_ref, dv_ref, dk_sum, dv_sum):
    step = pl.program_id(1)
    contract_last = (((1,), (1,)), ((), ()))
    contract_first = (((0,), (0,)), ((), ()))

    @pl.when(step == 0)
    def _():
        dk_sum[...] = jnp.zeros_like(dk_sum)
        dv_sum[...] = jnp.zeros_like(dv_sum)

    q, g, k, v = q_ref[0], g_ref[0], k_ref[0], v_ref[0]
    scores = lax.dot_general(q, k, contract_last, preferred_element_type=F32) * SCALE
    probs = jnp.exp(scores - log_ref[0])
    prob_grad = lax.dot_general(g, v, contract_last, preferred_element_type=F32)
    row_dot = jnp.sum(probs * prob_grad, axis=1, keepdims=True)
    score_grad = (probs * (prob_grad - row_dot)).astype(BF16)
    dq_ref[0] = (jnp.dot(score_grad, k, preferred_element_type=F32) * SCALE).astype(BF16)
    dk_sum[...] += lax.dot_general(score_grad, q, contract_first, preferred_element_type=F32)
    dv_sum[...] += lax.dot_general(
        probs.astype(BF16), g, contract_first, preferred_element_type=F32
    )

    @pl.when(step == pl.num_programs(1) - 1)
    def _():
        dk_ref[0] = (dk_sum[...] * SCALE).astype(BF16)
        dv_ref[0] = dv_sum[...].astype(BF16)


def attend_back(q, k, v, log, g, block):
    heads, frames, width = q.shape
    some = pl.BlockSpec((1, block, width), lambda h, i: (h, i, 0))
    every = pl.BlockSpec((1, frames, width), lambda h, i: (h, 0, 0))
    thin = pl.BlockSpec((1, block, 1), lambda h, i: (h, i, 0))
    return pl.pallas_call(
        attend_back_kernel,
        grid=(heads, frames // block),
        out_shape=(jax.ShapeDtypeStruct(q.shape, BF16),) * 3,
        in_specs=[some, some, thin, every, every],
        out_specs=(some, every, every),
        scratch_shapes=[pltpu.VMEM((frames, width), F32)] * 2,
        compiler_params=pltpu.CompilerParams(vmem_limit_bytes=VMEM_LIMIT),
    )(q, g, log, k, v)


def pad_rows(array, rows, axis):
    extra = rows - array.shape[axis]
    if extra == 0:
        return array
    widths = [(0, 0)] * array.ndim
    widths[axis] = (0, extra)
    return jnp.pad(array, widths)


def body(dp, inputs, cotangent, qkv_weight, proj_weight, up_weight, down_weight, qv_bias, up_bias, norm_gains, row_biases):
    zs = dp // 2
    rows, width = inputs.shape
    share = qkv_weight.shape[1]
    padded = -(-share // 16) * 16
    columns = qkv_weight.shape[2]
    hidden_width = up_weight.shape[1]
    heads = columns // HD
    frames = rows * TENSOR

    def wide(array):
        array = array.reshape(array.shape[0], -1)
        return jnp.pad(array, ((0, 0), (0, 128 - array.shape[1])))

    wa = jnp.concatenate([qkv_weight[0], qkv_weight[1], qkv_weight[2], proj_weight.T], axis=1)
    wb = jnp.concatenate([up_weight, down_weight.T], axis=1)
    bit = norm_gains.shape[1]
    small = jnp.concatenate(
        [wide(norm_gains), wide(row_biases), wide(qv_bias), wide(up_bias[None])], axis=0
    )
    small = pad_rows(small, 16, 0)
    x_all, cot_all, wa_all, wb_all, small_all = gather_all(
        dp, inputs, cotangent, pad_rows(wa, padded, 0), pad_rows(wb, padded, 0), small
    )

    def whole(array):
        return array[:, :, :share].reshape(width, array.shape[3])

    def split(array):
        return pad_rows(array.reshape(zs, 2, share, array.shape[1]), padded, 2)

    x_all = x_all.reshape(frames, width)
    cot_all = cot_all.reshape(frames, width)
    wa_all, wb_all = whole(wa_all), whole(wb_all)
    qkv_full, proj_t = wa_all[:, : 3 * columns], wa_all[:, 3 * columns :]
    up_full, down_t = wb_all[:, :hidden_width], wb_all[:, hidden_width:]
    small_all = small_all.astype(F32)
    tensor = lax.axis_index("tensor")
    vec = small_all[:, :, 0:8, :bit].transpose(2, 0, 1, 3).reshape(8, width)
    mine = lax.dynamic_index_in_dim(small_all, tensor, 1, keepdims=False)
    bits = qv_bias.shape[1]
    qv_full = mine[:, 6:8, :bits].transpose(1, 0, 2).reshape(2, columns)
    up_bias_full = mine[:, 8, : up_bias.shape[0]].reshape(hidden_width)

    normed = layer_norm(x_all.astype(F32), vec[0:1], vec[2:3]).astype(BF16)
    bias_row = jnp.concatenate([qv_full[0], jnp.zeros_like(qv_full[0]), qv_full[1]])
    projected = (jnp.dot(normed, qkv_full, preferred_element_type=F32) + bias_row).astype(BF16)
    split_qkv = projected.reshape(frames, 3, heads, HD).transpose(1, 2, 0, 3)
    head_q, head_k, head_v = split_qkv[0], split_qkv[1], split_qkv[2]

    def join_heads(stacked):
        return stacked.transpose(1, 0, 2).reshape(frames, columns)

    mixture, logsum = attend(head_q, head_k, head_v, min(512, frames))
    attended = join_heads(mixture)
    contract_last = (((1,), (1,)), ((), ()))
    contract_first = (((0,), (0,)), ((), ()))

    def blocks(array):
        return array.reshape(TENSOR, rows, width)

    branch = lax.dot_general(attended, proj_t, contract_last, preferred_element_type=F32)
    middle, normed_two = make_middle(dp, blocks(branch.astype(BF16)), inputs, vec)
    normed_two = normed_two.reshape(frames, width)
    hidden = jnp.dot(normed_two, up_full, preferred_element_type=F32) + up_bias_full
    cumulative = 0.5 * (1.0 + jax.scipy.special.erf(hidden * ROOT_HALF))
    activated = (hidden * cumulative).astype(BF16)
    slope = cumulative + hidden * jnp.exp(-0.5 * hidden * hidden) * ROOT_TWO_PI_INVERSE
    act_grad = jnp.dot(cot_all, down_t, preferred_element_type=F32)
    hidden_grad = (act_grad * slope).astype(BF16)
    grad_part = lax.dot_general(hidden_grad, up_full, contract_last, preferred_element_type=F32)
    feed_part = lax.dot_general(activated, down_t, contract_last, preferred_element_type=F32)
    outputs, middle_grad, attn_grad, sums = go_back(
        dp, blocks(grad_part.astype(BF16)), blocks(feed_part.astype(BF16)), middle, cotangent, vec
    )
    up_bias_grad = jnp.sum(hidden_grad.astype(F32), axis=0)
    up_grad = lax.dot_general(normed_two, hidden_grad, contract_first, preferred_element_type=F32)
    down_grad = lax.dot_general(cot_all, activated, contract_first, preferred_element_type=F32)
    attn_grad = attn_grad.reshape(frames, width)
    proj_grad = lax.dot_general(attn_grad, attended, contract_first, preferred_element_type=F32)
    attended_grad = jnp.dot(attn_grad, proj_t, preferred_element_type=F32).astype(BF16)
    head_g = attended_grad.reshape(frames, heads, HD).transpose(1, 0, 2)
    head_dq, head_dk, head_dv = attend_back(
        head_q, head_k, head_v, logsum, head_g, min(512, frames)
    )
    stacked = jnp.concatenate([join_heads(head_dq), join_heads(head_dk), join_heads(head_dv)], axis=1)
    qkv_grad = lax.dot_general(normed, stacked, contract_first, preferred_element_type=F32)
    column_sums = jnp.sum(stacked.astype(F32), axis=0)
    normed_part = lax.dot_general(stacked, qkv_full, contract_last, preferred_element_type=F32)
    own_sums = jnp.zeros((8, width), F32)
    own_sums = own_sums.at[0, :hidden_width].set(up_bias_grad)
    own_sums = own_sums.at[1, :columns].set(column_sums[:columns])
    own_sums = own_sums.at[2, :columns].set(column_sums[2 * columns :])
    ga = jnp.concatenate([qkv_grad, proj_grad], axis=1).astype(BF16)
    gb = jnp.concatenate([up_grad, down_grad], axis=1).astype(BF16)
    input_grad, ga_out, gb_out, all_sums = finish_all(
        dp, blocks(normed_part.astype(BF16)), inputs, middle_grad, vec, sums, own_sums, split(ga), split(gb)
    )
    ga_out, gb_out = ga_out[:share], gb_out[:share]
    place = lax.axis_index("dp")
    both = place * TENSOR + tensor
    qkv_grad_out = ga_out[:, : 3 * columns].reshape(share, 3, columns).transpose(1, 0, 2)
    vectors = lax.dynamic_slice(all_sums, (0, both * bit), (6, bit))
    qv_out = lax.dynamic_slice(all_sums, (9, place * bits), (2, bits))
    up_bits = up_bias.shape[0]
    up_bias_out = lax.dynamic_slice(all_sums, (8, place * up_bits), (1, up_bits))[0]
    return (
        outputs,
        input_grad,
        qkv_grad_out,
        ga_out[:, 3 * columns :].T,
        gb_out[:, :hidden_width],
        gb_out[:, hidden_width:].T,
        qv_out,
        up_bias_out,
        vectors[0:2],
        vectors[2:6],
    )


def solution(mesh):
    both = ("dp", "tensor")
    placed = (
        P(both, None),
        P(both, None),
        P(None, "dp", "tensor"),
        P("tensor", "dp"),
        P("dp", "tensor"),
        P("tensor", "dp"),
        P(None, ("tensor", "dp")),
        P(("tensor", "dp")),
        P(None, both),
        P(None, both),
    )
    return jax.shard_map(
        functools.partial(body, mesh.shape["dp"]),
        mesh=mesh,
        in_specs=placed,
        out_specs=(
            P(both, None),
            P(both, None),
            P(None, "dp", "tensor"),
            P("tensor", "dp"),
            P("dp", "tensor"),
            P("tensor", "dp"),
            P(None, ("tensor", "dp")),
            P(("tensor", "dp")),
            P(None, both),
            P(None, both),
        ),
        check_vma=False,
    )
```

```python
import functools

import jax
import jax.numpy as jnp
from jax import lax
from jax.experimental import pallas as pl
from jax.experimental.pallas import tpu as pltpu
from jax.sharding import PartitionSpec as P

HD = 64
EPSILON = 1e-05
SCALE = 0.125
ROOT_HALF = 0.7071067811865476
ROOT_TWO_PI_INVERSE = 0.3989422804014327
F32 = jnp.float32
BF16 = jnp.bfloat16
VMEM_LIMIT = 50 * 1024 * 1024
MESH = pl.DeviceIdType.MESH
TENSOR = 4


def layer_norm(values, gain_row, shift_row):
    center = values - jnp.mean(values, axis=-1, keepdims=True)
    spread = jnp.mean(center * center, axis=-1, keepdims=True)
    return center * lax.rsqrt(spread + EPSILON) * gain_row + shift_row


def norm_back(values, gain_row, incoming):
    center = values - jnp.mean(values, axis=-1, keepdims=True)
    spread = jnp.mean(center * center, axis=-1, keepdims=True)
    inverse = lax.rsqrt(spread + EPSILON)
    unit_rows = center * inverse
    scaled = incoming * gain_row
    grad_in = inverse * (
        scaled
        - jnp.mean(scaled, axis=-1, keepdims=True)
        - unit_rows * jnp.mean(scaled * unit_rows, axis=-1, keepdims=True)
    )
    return (
        grad_in,
        jnp.sum(incoming * unit_rows, axis=0, keepdims=True),
        jnp.sum(incoming, axis=0, keepdims=True),
    )


class Place:
    def __init__(self, dp):
        self.dp = dp
        self.zs = dp // 2
        self.d = lax.axis_index("dp")
        self.t = lax.axis_index("tensor")
        self.z = self.d // 2
        self.x = lax.rem(self.d, 2)
        self.core = self.t + 1 - 2 * lax.rem(self.t, 2)
        self.across = lax.rem(self.t + 2, TENSOR)
        self.diagonal = lax.rem(self.core + 2, TENSOR)

    def tensor_id(self, t):
        return {"dp": self.d, "tensor": t}

    def dp_id(self, d):
        return {"dp": d, "tensor": self.t}

    def x_id(self):
        return self.dp_id(self.z * 2 + 1 - self.x)

    def z_of(self, k):
        return lax.rem(self.z + k, self.zs)

    def z_from(self, k):
        return lax.rem(self.z + self.zs - k, self.zs)

    def z_id(self, k):
        return self.dp_id(self.z_of(k) * 2 + self.x)


def greet(peers):
    barrier = pltpu.get_barrier_semaphore()
    for peer in peers:
        pl.semaphore_signal(barrier, inc=1, device_id=peer, device_id_type=MESH)
    pl.semaphore_wait(barrier, len(peers))


def remote(src, dst, send, recv, peer):
    return pltpu.make_async_remote_copy(
        src_ref=src, dst_ref=dst, send_sem=send, recv_sem=recv, device_id=peer, device_id_type=MESH
    )


class TensorGather:
    def __init__(self, here, own, out, send, recv):
        t = here.t
        self.first = [
            remote(own, out.at[t], send.at[0], recv.at[0], here.tensor_id(here.across)),
            remote(own, out.at[t], send.at[1], recv.at[1], here.tensor_id(here.core)),
        ]
        landed = out.at[here.across]
        self.relay = remote(landed, landed, send.at[2], recv.at[2], here.tensor_id(here.core))

    def start(self):
        for copy in self.first:
            copy.start()

    def pass_on(self):
        self.first[0].wait_recv()
        self.relay.start()

    def finish(self):
        self.first[1].wait_recv()
        self.relay.wait_recv()
        self.first[0].wait_send()
        self.first[1].wait_send()
        self.relay.wait_send()


class TensorScatter:
    def __init__(self, here, part, from_core, to_across, from_across, send, recv):
        self.here, self.part = here, part
        self.from_core, self.to_across, self.from_across = from_core, to_across, from_across
        core = here.tensor_id(here.core)
        self.far = remote(part.at[here.diagonal], from_core.at[0], send.at[0], recv.at[0], core)
        self.near = remote(part.at[here.core], from_core.at[1], send.at[1], recv.at[1], core)
        self.cross = remote(
            to_across, from_across, send.at[2], recv.at[2], here.tensor_id(here.across)
        )

    def start(self):
        self.far.start()
        self.near.start()

    def pass_on(self):
        self.far.wait_recv()
        total = self.part[self.here.across].astype(F32) + self.from_core[0].astype(F32)
        self.to_across[...] = total.astype(BF16)
        self.cross.start()

    def result(self):
        self.near.wait_recv()
        total = self.part[self.here.t].astype(F32) + self.from_core[1].astype(F32)
        self.cross.wait_recv()
        return total + self.from_across[...].astype(F32)

    def finish(self):
        self.far.wait_send()
        self.near.wait_send()
        self.cross.wait_send()


def scatter_scratch(rows, width):
    return [
        pltpu.VMEM((2, rows, width), BF16),
        pltpu.VMEM((rows, width), BF16),
        pltpu.VMEM((rows, width), BF16),
        pltpu.SemaphoreType.DMA((3,)),
        pltpu.SemaphoreType.DMA((3,)),
    ]


class WeightGather:
    def __init__(self, here, own, out, sz, rz, sx, rx, local):
        self.zs = here.zs
        mine = out.at[here.z, here.x]
        self.keep = pltpu.make_async_copy(own, mine, local)
        self.along = [None] + [
            remote(own, mine, sz.at[k], rz.at[k], here.z_id(k)) for k in range(1, self.zs)
        ]
        self.over = [remote(own, mine, sx.at[0], rx.at[0], here.x_id())]
        for k in range(1, self.zs):
            landed = out.at[here.z_from(k), here.x]
            self.over.append(remote(landed, landed, sx.at[k], rx.at[k], here.x_id()))

    def start(self):
        self.along[1].start()
        self.over[0].start()
        self.keep.start()

    def launch(self, k):
        self.along[k].start()

    def pass_on(self, k):
        self.along[k].wait_recv()
        self.over[k].start()

    def finish(self):
        for copy in self.over:
            copy.wait_recv()
        for copy in self.along[1:] + self.over:
            copy.wait_send()
        self.keep.wait()


def weight_sems(zs):
    return [pltpu.SemaphoreType.DMA((zs,))] * 4 + [pltpu.SemaphoreType.DMA]


class GradScatter:
    def __init__(self, here, part, from_x, to_z, from_z, sz, rz, sx, rx):
        self.here, self.part = here, part
        self.from_x, self.to_z, self.from_z = from_x, to_z, from_z
        self.order = list(range(1, here.zs)) + [0]
        self.over, self.along = {}, {}
        for k in self.order:
            slot = here.z_of(k)
            self.over[k] = remote(
                part.at[slot, 1 - here.x], from_x.at[k], sx.at[k], rx.at[k], here.x_id()
            )
            if k:
                self.along[k] = remote(to_z.at[k], from_z.at[k], sz.at[k], rz.at[k], here.z_id(k))

    def launch(self, k):
        self.over[k].start()

    def half(self, k):
        here = self.here
        self.over[k].wait_recv()
        return self.part[here.z_of(k), here.x].astype(F32) + self.from_x[k].astype(F32)

    def pass_on(self, k):
        self.to_z[k] = self.half(k).astype(BF16)
        self.along[k].start()

    def result(self):
        total = self.half(0)
        for k in range(1, self.here.zs):
            self.along[k].wait_recv()
            total = total + self.from_z[k].astype(F32)
        return total

    def finish(self):
        for k in self.order:
            self.over[k].wait_send()
            if k:
                self.along[k].wait_send()


def grad_scratch(zs, rows, width):
    return [pltpu.VMEM((zs, rows, width), BF16)] * 3 + [pltpu.SemaphoreType.DMA((zs,))] * 4


def tensor_peers(here):
    return [here.tensor_id(t) for t in (here.core, here.across, here.diagonal)]


def dp_peers(here):
    return [here.dp_id(lax.rem(here.d + k, here.dp)) for k in range(1, here.dp)]


def gather_kernel(dp, x_ref, wa_ref, s_ref, x_out, wa_out, s_out, *sems):
    here = Place(dp)
    gx = sems[0:2]
    wa = sems[2:7]
    st_send, st_recv, sd_send, sd_recv, local = sems[7:12]
    greet(tensor_peers(here) + dp_peers(here))
    keeps = [
        pltpu.make_async_copy(x_ref, x_out.at[here.t], local.at[0]),
        pltpu.make_async_copy(s_ref, s_out.at[here.d, here.t], local.at[1]),
    ]
    small = [
        remote(s_ref, s_out.at[here.d, here.t], st_send.at[i], st_recv.at[i], peer)
        for i, peer in enumerate(tensor_peers(here))
    ]
    for copy in small:
        copy.start()
    keeps[1].start()
    a_gather = WeightGather(here, wa_ref, wa_out, *wa)
    a_gather.start()
    x_gather = TensorGather(here, x_ref, x_out, *gx)
    x_gather.start()
    keeps[0].start()
    for copy in small:
        copy.wait_recv()
    keeps[1].wait()
    row = s_out.at[here.d]
    spread = [
        remote(row, row, sd_send.at[k], sd_recv.at[k], here.dp_id(lax.rem(here.d + k, dp)))
        for k in range(1, dp)
    ]
    for copy in spread:
        copy.start()
    for k in range(1, here.zs):
        if k + 1 < here.zs:
            a_gather.launch(k + 1)
        a_gather.pass_on(k)
        if k == 1:
            x_gather.pass_on()
    x_gather.finish()
    a_gather.finish()
    for copy in spread:
        copy.wait_recv()
    for copy in small + spread:
        copy.wait_send()
    keeps[0].wait()


def gather_all(dp, x, wa, small):
    zs = dp // 2
    anywhere = pl.BlockSpec(memory_space=pl.ANY)
    dma = pltpu.SemaphoreType.DMA
    shape = jax.ShapeDtypeStruct
    return pl.pallas_call(
        functools.partial(gather_kernel, dp),
        out_shape=(
            shape((TENSOR,) + x.shape, BF16),
            shape((zs, 2) + wa.shape, BF16),
            shape((dp, TENSOR) + small.shape, BF16),
        ),
        in_specs=[anywhere] * 3,
        out_specs=(anywhere,) * 3,
        scratch_shapes=[dma((3,))] * 2
        + weight_sems(zs)
        + [dma((3,)), dma((3,)), dma((dp,)), dma((dp,)), dma((2,))],
        compiler_params=pltpu.CompilerParams(
            collective_id=0, has_side_effects=True, vmem_limit_bytes=VMEM_LIMIT
        ),
    )(x, wa, small)


LAST = (((1,), (1,)), ((), ()))
FIRST = (((0,), (0,)), ((), ()))


def block_rows(here, j, rows):
    return pl.ds(pl.multiple_of(j * rows, rows), rows)


def middle_kernel(
    dp, qkv, proj_t, x_ref, vec, c_ref, wb_ref,
    middle_out, two_out, mix_out, log_out, c_out, wb_out, part, *rest
):
    here = Place(dp)
    rows = x_ref.shape[0]
    columns = proj_t.shape[1]
    scatter = TensorScatter(here, part, *rest[0:5])
    gather = TensorGather(here, two_out.at[here.t], two_out, *rest[5:7])
    c_gather = TensorGather(here, c_ref, c_out, *rest[7:9])
    b_gather = WeightGather(here, wb_ref, wb_out, *rest[9:14])
    keep = pltpu.make_async_copy(c_ref, c_out.at[here.t], rest[14])

    def attend(j):
        at = block_rows(here, j, rows)
        for h in range(columns // HD):
            low, high = h * HD, (h + 1) * HD
            q = qkv[at, low:high]
            k = qkv[:, columns + low : columns + high]
            v = qkv[:, 2 * columns + low : 2 * columns + high]
            scores = lax.dot_general(q, k, LAST, preferred_element_type=F32) * SCALE
            top = jnp.max(scores, axis=1, keepdims=True)
            exponent = jnp.exp(scores - top)
            total = jnp.sum(exponent, axis=1, keepdims=True)
            probs = (exponent * (1.0 / total)).astype(BF16)
            mix_out[at, low:high] = jnp.dot(probs, v, preferred_element_type=F32).astype(BF16)
            log_out[at, h : h + 1] = top + jnp.log(total)
        part[j] = lax.dot_general(
            mix_out[at, :], proj_t[...], LAST, preferred_element_type=F32
        ).astype(BF16)

    greet(tensor_peers(here) + dp_peers(here))
    b_gather.start()
    attend(here.diagonal)
    scatter.far.start()
    attend(here.core)
    scatter.near.start()
    for k in range(2, here.zs):
        b_gather.launch(k)
    b_gather.pass_on(1)
    attend(here.across)
    scatter.pass_on()
    c_gather.start()
    keep.start()
    attend(here.t)
    middle = x_ref[...].astype(F32) + scatter.result() + vec[3:4]
    middle_out[...] = middle
    two_out[here.t] = layer_norm(middle, vec[1:2], vec[4:5]).astype(BF16)
    gather.start()
    b_gather.pass_on(2)
    c_gather.pass_on()
    gather.pass_on()
    for k in range(3, here.zs):
        b_gather.pass_on(k)
    gather.finish()
    scatter.finish()
    c_gather.finish()
    b_gather.finish()
    keep.wait()


def make_middle(dp, qkv, proj_t, x, vec, cot, wb):
    zs = dp // 2
    vmem = pl.BlockSpec(memory_space=pltpu.VMEM)
    anywhere = pl.BlockSpec(memory_space=pl.ANY)
    rows, width = x.shape
    frames, columns = qkv.shape[0], proj_t.shape[1]
    dma = pltpu.SemaphoreType.DMA
    shape = jax.ShapeDtypeStruct
    return pl.pallas_call(
        functools.partial(middle_kernel, dp),
        out_shape=(
            shape((rows, width), F32),
            shape((TENSOR, rows, width), BF16),
            shape((frames, columns), BF16),
            shape((frames, 128), F32),
            shape((TENSOR, rows, width), BF16),
            shape((zs, 2) + wb.shape, BF16),
        ),
        in_specs=[vmem] * 4 + [anywhere] * 2,
        out_specs=(vmem,) * 4 + (anywhere,) * 2,
        scratch_shapes=[pltpu.VMEM((TENSOR, rows, width), BF16)]
        + scatter_scratch(rows, width)
        + [dma((3,))] * 4
        + weight_sems(zs)
        + [dma],
        compiler_params=pltpu.CompilerParams(
            collective_id=1, has_side_effects=True, vmem_limit_bytes=VMEM_LIMIT
        ),
    )(qkv, proj_t, x, vec, cot, wb)


def back_kernel(
    dp, grad_part, feed_part, middle, cot, vec, qkv, proj_t, log, gb,
    out, mgrad_out, attn_out, sums, grads, gb_out, dk_sum, dv_sum, *rest
):
    here = Place(dp)
    rows = cot.shape[0]
    columns = proj_t.shape[1]
    heads = columns // HD
    grad_scatter = TensorScatter(here, grad_part, *rest[0:5])
    feed_scatter = TensorScatter(here, feed_part, *rest[5:10])
    gather = TensorGather(here, attn_out.at[here.t], attn_out, *rest[10:12])
    b_scatter = GradScatter(here, gb, *rest[12:19])

    def attend_back(j, first):
        at = block_rows(here, j, rows)
        mixed = jnp.dot(attn_out[j], proj_t[...], preferred_element_type=F32).astype(BF16)
        for h in range(heads):
            low, high = h * HD, (h + 1) * HD
            g = mixed[:, low:high]
            q = qkv[at, low:high]
            k = qkv[:, columns + low : columns + high]
            v = qkv[:, 2 * columns + low : 2 * columns + high]
            scores = lax.dot_general(q, k, LAST, preferred_element_type=F32) * SCALE
            probs = jnp.exp(scores - log[at, h : h + 1])
            prob_grad = lax.dot_general(g, v, LAST, preferred_element_type=F32)
            row_dot = jnp.sum(probs * prob_grad, axis=1, keepdims=True)
            score_grad = (probs * (prob_grad - row_dot)).astype(BF16)
            grads[at, low:high] = (
                jnp.dot(score_grad, k, preferred_element_type=F32) * SCALE
            ).astype(BF16)
            dk = lax.dot_general(score_grad, q, FIRST, preferred_element_type=F32)
            dv = lax.dot_general(probs.astype(BF16), g, FIRST, preferred_element_type=F32)
            if first:
                dk_sum[h] = dk
                dv_sum[h] = dv
            else:
                dk_sum[h] += dk
                dv_sum[h] += dv

    greet(tensor_peers(here) + dp_peers(here))
    grad_scatter.start()
    b_scatter.launch(1)
    if here.zs > 2:
        b_scatter.launch(2)
    grad_scatter.pass_on()
    feed_scatter.start()
    incoming = grad_scatter.result()
    mid = middle[...]
    mid_part, gain_sum, shift_sum = norm_back(mid, vec[1:2], incoming)
    grad_out = cot[...].astype(F32)
    mgrad = grad_out + mid_part
    attn_out[here.t] = mgrad.astype(BF16)
    gather.start()
    for k in range(3, here.zs):
        b_scatter.launch(k)
    b_scatter.launch(0)
    mgrad_out[...] = mgrad
    sums[0:1] = gain_sum
    sums[1:2] = jnp.sum(mgrad, axis=0, keepdims=True)
    sums[2:3] = shift_sum
    sums[3:4] = jnp.sum(grad_out, axis=0, keepdims=True)
    b_scatter.pass_on(1)
    attend_back(here.t, True)
    if here.zs > 2:
        b_scatter.pass_on(2)
    gather.pass_on()
    feed_scatter.pass_on()
    gather.first[1].wait_recv()
    attend_back(here.core, False)
    attend_back(here.across, False)
    for k in range(3, here.zs):
        b_scatter.pass_on(k)
    gather.relay.wait_recv()
    attend_back(here.diagonal, False)
    for h in range(heads):
        low, high = h * HD, (h + 1) * HD
        grads[:, columns + low : columns + high] = (dk_sum[h] * SCALE).astype(BF16)
        grads[:, 2 * columns + low : 2 * columns + high] = dv_sum[h].astype(BF16)
    out[...] = (mid + feed_scatter.result() + vec[5:6]).astype(BF16)
    gb_out[...] = b_scatter.result()
    for copy in gather.first + [gather.relay]:
        copy.wait_send()
    grad_scatter.finish()
    feed_scatter.finish()
    b_scatter.finish()


def go_back(dp, grad_part, feed_part, middle, cot, vec, qkv, proj_t, log, gb):
    zs = dp // 2
    vmem = pl.BlockSpec(memory_space=pltpu.VMEM)
    rows, width = cot.shape
    heads = proj_t.shape[1] // HD
    dma = pltpu.SemaphoreType.DMA
    shape = jax.ShapeDtypeStruct
    return pl.pallas_call(
        functools.partial(back_kernel, dp),
        out_shape=(
            shape((rows, width), BF16),
            shape((rows, width), F32),
            shape((TENSOR, rows, width), BF16),
            shape((4, width), F32),
            shape(qkv.shape, BF16),
            shape(gb.shape[2:], F32),
        ),
        in_specs=[vmem] * 9,
        out_specs=(vmem,) * 6,
        scratch_shapes=[pltpu.VMEM((heads, qkv.shape[0], HD), F32)] * 2
        + scatter_scratch(rows, width) * 2
        + [dma((3,)), dma((3,))]
        + grad_scratch(zs, *gb.shape[2:]),
        compiler_params=pltpu.CompilerParams(
            collective_id=2, has_side_effects=True, vmem_limit_bytes=VMEM_LIMIT
        ),
    )(grad_part, feed_part, middle, cot, vec, qkv, proj_t, log, gb)


def last_kernel(
    dp, part, x_ref, mgrad, vec, sums, own_sums, ga, in_out, ga_out, sum_out, *rest
):
    here = Place(dp)
    scatter = TensorScatter(here, part, *rest[0:5])
    a_scatter = GradScatter(here, ga, *rest[5:12])
    near, around, st_send, st_recv, sd_send, sd_recv = rest[12:18]
    greet(tensor_peers(here) + dp_peers(here))
    scatter.start()
    a_scatter.launch(1)
    if here.zs > 2:
        a_scatter.launch(2)
    scatter.pass_on()
    a_scatter.pass_on(1)
    for k in range(3, here.zs):
        a_scatter.launch(k)
    a_scatter.launch(0)
    if here.zs > 2:
        a_scatter.pass_on(2)
    x = x_ref[...].astype(F32)
    in_part, gain_sum, shift_sum = norm_back(x, vec[0:1], scatter.result())
    in_out[...] = mgrad[...] + in_part
    near[0, 0:1] = gain_sum
    near[0, 1:2] = sums[0:1]
    near[0, 2:3] = shift_sum
    near[0, 3:6] = sums[1:4]
    near[0, 6:8] = jnp.zeros_like(near[0, 6:8])
    small = [
        remote(near.at[0], near.at[i + 1], st_send.at[i], st_recv.at[i], peer)
        for i, peer in enumerate(tensor_peers(here))
    ]
    for copy in small:
        copy.start()
    for k in range(3, here.zs):
        a_scatter.pass_on(k)
    for copy in small:
        copy.wait_recv()
    around[0, 0:8] = (near[0] + near[1]) + (near[2] + near[3])
    around[0, 8:16] = own_sums[...]
    spread = [
        remote(
            around.at[0], around.at[k], sd_send.at[k], sd_recv.at[k],
            here.dp_id(lax.rem(here.d + k, dp)),
        )
        for k in range(1, dp)
    ]
    for copy in spread:
        copy.start()
    ga_out[...] = a_scatter.result()
    total = around[0]
    for k in range(1, dp):
        spread[k - 1].wait_recv()
        total = total + around[k]
    sum_out[...] = total
    scatter.finish()
    a_scatter.finish()
    for copy in small + spread:
        copy.wait_send()


def finish_all(dp, part, x, mgrad, vec, sums, own_sums, ga):
    zs = dp // 2
    vmem = pl.BlockSpec(memory_space=pltpu.VMEM)
    rows, width = x.shape
    dma = pltpu.SemaphoreType.DMA
    shape = jax.ShapeDtypeStruct
    return pl.pallas_call(
        functools.partial(last_kernel, dp),
        out_shape=(
            shape((rows, width), F32),
            shape(ga.shape[2:], F32),
            shape((16, width), F32),
        ),
        in_specs=[vmem] * 7,
        out_specs=(vmem,) * 3,
        scratch_shapes=scatter_scratch(rows, width)
        + grad_scratch(zs, *ga.shape[2:])
        + [pltpu.VMEM((TENSOR, 8, width), F32), pltpu.VMEM((dp, 16, width), F32)]
        + [dma((3,)), dma((3,)), dma((dp,)), dma((dp,))],
        compiler_params=pltpu.CompilerParams(
            collective_id=3, has_side_effects=True, vmem_limit_bytes=VMEM_LIMIT
        ),
    )(part, x, mgrad, vec, sums, own_sums, ga)


def pad_rows(array, rows, axis):
    extra = rows - array.shape[axis]
    if extra == 0:
        return array
    widths = [(0, 0)] * array.ndim
    widths[axis] = (0, extra)
    return jnp.pad(array, widths)


def body(dp, inputs, cotangent, qkv_weight, proj_weight, up_weight, down_weight, qv_bias, up_bias, norm_gains, row_biases):
    zs = dp // 2
    rows, width = inputs.shape
    share = qkv_weight.shape[1]
    padded = -(-share // 16) * 16
    columns = qkv_weight.shape[2]
    hidden_width = up_weight.shape[1]
    heads = columns // HD
    frames = rows * TENSOR

    def wide(array):
        array = array.reshape(array.shape[0], -1)
        return jnp.pad(array, ((0, 0), (0, 128 - array.shape[1])))

    wa = jnp.concatenate([qkv_weight[0], qkv_weight[1], qkv_weight[2], proj_weight.T], axis=1)
    wb = jnp.concatenate([up_weight, down_weight.T], axis=1)
    bit = norm_gains.shape[1]
    small = jnp.concatenate(
        [wide(norm_gains), wide(row_biases), wide(qv_bias), wide(up_bias[None])], axis=0
    )
    small = pad_rows(small, 16, 0)
    x_all, wa_all, small_all = gather_all(dp, inputs, pad_rows(wa, padded, 0), small)

    def whole(array):
        return array[:, :, :share].reshape(width, array.shape[3])

    def split(array):
        return pad_rows(array.reshape(zs, 2, share, array.shape[1]), padded, 2)

    x_all = x_all.reshape(frames, width)
    wa_all = whole(wa_all)
    qkv_full, proj_t = wa_all[:, : 3 * columns], wa_all[:, 3 * columns :]
    small_all = small_all.astype(F32)
    tensor = lax.axis_index("tensor")
    vec = small_all[:, :, 0:8, :bit].transpose(2, 0, 1, 3).reshape(8, width)
    mine = lax.dynamic_index_in_dim(small_all, tensor, 1, keepdims=False)
    bits = qv_bias.shape[1]
    qv_full = mine[:, 6:8, :bits].transpose(1, 0, 2).reshape(2, columns)
    up_bias_full = mine[:, 8, : up_bias.shape[0]].reshape(hidden_width)

    normed = layer_norm(x_all.astype(F32), vec[0:1], vec[2:3]).astype(BF16)
    bias_row = jnp.concatenate([qv_full[0], jnp.zeros_like(qv_full[0]), qv_full[1]])
    projected = (jnp.dot(normed, qkv_full, preferred_element_type=F32) + bias_row).astype(BF16)

    def blocks(array):
        return array.reshape(TENSOR, rows, width)

    middle, normed_two, attended, logsum, cot_all, wb_all = make_middle(
        dp, projected, proj_t, inputs, vec, cotangent, pad_rows(wb, padded, 0)
    )
    normed_two = normed_two.reshape(frames, width)
    cot_all = cot_all.reshape(frames, width)
    wb_all = whole(wb_all)
    up_full, down_t = wb_all[:, :hidden_width], wb_all[:, hidden_width:]
    hidden = jnp.dot(normed_two, up_full, preferred_element_type=F32) + up_bias_full
    cumulative = 0.5 * (1.0 + jax.scipy.special.erf(hidden * ROOT_HALF))
    activated = (hidden * cumulative).astype(BF16)
    slope = cumulative + hidden * jnp.exp(-0.5 * hidden * hidden) * ROOT_TWO_PI_INVERSE
    act_grad = jnp.dot(cot_all, down_t, preferred_element_type=F32)
    hidden_grad = (act_grad * slope).astype(BF16)
    grad_part = lax.dot_general(hidden_grad, up_full, LAST, preferred_element_type=F32)
    feed_part = lax.dot_general(activated, down_t, LAST, preferred_element_type=F32)
    up_bias_grad = jnp.sum(hidden_grad.astype(F32), axis=0)
    up_grad = lax.dot_general(normed_two, hidden_grad, FIRST, preferred_element_type=F32)
    down_grad = lax.dot_general(cot_all, activated, FIRST, preferred_element_type=F32)
    gb = jnp.concatenate([up_grad, down_grad], axis=1).astype(BF16)
    outputs, middle_grad, attn_grad, sums, stacked, gb_out = go_back(
        dp, blocks(grad_part.astype(BF16)), blocks(feed_part.astype(BF16)), middle, cotangent, vec,
        projected, proj_t, logsum, split(gb),
    )
    attn_grad = attn_grad.reshape(frames, width)
    proj_grad = lax.dot_general(attn_grad, attended, FIRST, preferred_element_type=F32)
    qkv_grad = lax.dot_general(normed, stacked, FIRST, preferred_element_type=F32)
    column_sums = jnp.sum(stacked.astype(F32), axis=0)
    normed_part = lax.dot_general(stacked, qkv_full, LAST, preferred_element_type=F32)
    own_sums = jnp.zeros((8, width), F32)
    own_sums = own_sums.at[0, :hidden_width].set(up_bias_grad)
    own_sums = own_sums.at[1, :columns].set(column_sums[:columns])
    own_sums = own_sums.at[2, :columns].set(column_sums[2 * columns :])
    ga = jnp.concatenate([qkv_grad, proj_grad], axis=1).astype(BF16)
    input_grad, ga_out, all_sums = finish_all(
        dp, blocks(normed_part.astype(BF16)), inputs, middle_grad, vec, sums, own_sums, split(ga)
    )
    ga_out, gb_out = ga_out[:share], gb_out[:share]
    place = lax.axis_index("dp")
    both = place * TENSOR + tensor
    qkv_grad_out = ga_out[:, : 3 * columns].reshape(share, 3, columns).transpose(1, 0, 2)
    vectors = lax.dynamic_slice(all_sums, (0, both * bit), (6, bit))
    qv_out = lax.dynamic_slice(all_sums, (9, place * bits), (2, bits))
    up_bits = up_bias.shape[0]
    up_bias_out = lax.dynamic_slice(all_sums, (8, place * up_bits), (1, up_bits))[0]
    return (
        outputs,
        input_grad,
        qkv_grad_out,
        ga_out[:, 3 * columns :].T,
        gb_out[:, :hidden_width],
        gb_out[:, hidden_width:].T,
        qv_out,
        up_bias_out,
        vectors[0:2],
        vectors[2:6],
    )


def solution(mesh):
    both = ("dp", "tensor")
    placed = (
        P(both, None),
        P(both, None),
        P(None, "dp", "tensor"),
        P("tensor", "dp"),
        P("dp", "tensor"),
        P("tensor", "dp"),
        P(None, ("tensor", "dp")),
        P(("tensor", "dp")),
        P(None, both),
        P(None, both),
    )
    return jax.shard_map(
        functools.partial(body, mesh.shape["dp"]),
        mesh=mesh,
        in_specs=placed,
        out_specs=(
            P(both, None),
            P(both, None),
            P(None, "dp", "tensor"),
            P("tensor", "dp"),
            P("dp", "tensor"),
            P("tensor", "dp"),
            P(None, ("tensor", "dp")),
            P(("tensor", "dp")),
            P(None, both),
            P(None, both),
        ),
        check_vma=False,
    )
```

```python
import functools

import jax
import jax.numpy as jnp
from jax import lax
from jax.experimental import pallas as pl
from jax.experimental.pallas import tpu as pltpu
from jax.sharding import PartitionSpec as P

HD = 64
EPSILON = 1e-05
SCALE = 0.125
ROOT_HALF = 0.7071067811865476
ROOT_TWO_PI_INVERSE = 0.3989422804014327
F32 = jnp.float32
BF16 = jnp.bfloat16
VMEM_LIMIT = 50 * 1024 * 1024
MESH = pl.DeviceIdType.MESH
TENSOR = 4


def layer_norm(values, gain_row, shift_row):
    center = values - jnp.mean(values, axis=-1, keepdims=True)
    spread = jnp.mean(center * center, axis=-1, keepdims=True)
    return center * lax.rsqrt(spread + EPSILON) * gain_row + shift_row


def norm_back(values, gain_row, incoming):
    center = values - jnp.mean(values, axis=-1, keepdims=True)
    spread = jnp.mean(center * center, axis=-1, keepdims=True)
    inverse = lax.rsqrt(spread + EPSILON)
    unit_rows = center * inverse
    scaled = incoming * gain_row
    grad_in = inverse * (
        scaled
        - jnp.mean(scaled, axis=-1, keepdims=True)
        - unit_rows * jnp.mean(scaled * unit_rows, axis=-1, keepdims=True)
    )
    return (
        grad_in,
        jnp.sum(incoming * unit_rows, axis=0, keepdims=True),
        jnp.sum(incoming, axis=0, keepdims=True),
    )


class Place:
    def __init__(self, dp):
        self.dp = dp
        self.zs = dp // 2
        self.d = lax.axis_index("dp")
        self.t = lax.axis_index("tensor")
        self.z = self.d // 2
        self.x = lax.rem(self.d, 2)
        self.core = self.t + 1 - 2 * lax.rem(self.t, 2)
        self.across = lax.rem(self.t + 2, TENSOR)
        self.diagonal = lax.rem(self.core + 2, TENSOR)

    def tensor_id(self, t):
        return {"dp": self.d, "tensor": t}

    def dp_id(self, d):
        return {"dp": d, "tensor": self.t}

    def x_id(self):
        return self.dp_id(self.z * 2 + 1 - self.x)

    def z_of(self, k):
        return lax.rem(self.z + k, self.zs)

    def z_from(self, k):
        return lax.rem(self.z + self.zs - k, self.zs)

    def z_id(self, k):
        return self.dp_id(self.z_of(k) * 2 + self.x)


def greet(peers):
    barrier = pltpu.get_barrier_semaphore()
    for peer in peers:
        pl.semaphore_signal(barrier, inc=1, device_id=peer, device_id_type=MESH)
    pl.semaphore_wait(barrier, len(peers))


def remote(src, dst, send, recv, peer):
    return pltpu.make_async_remote_copy(
        src_ref=src, dst_ref=dst, send_sem=send, recv_sem=recv, device_id=peer, device_id_type=MESH
    )


class TensorGather:
    def __init__(self, here, own, out, send, recv):
        t = here.t
        self.first = [
            remote(own, out.at[t], send.at[0], recv.at[0], here.tensor_id(here.across)),
            remote(own, out.at[t], send.at[1], recv.at[1], here.tensor_id(here.core)),
        ]
        landed = out.at[here.across]
        self.relay = remote(landed, landed, send.at[2], recv.at[2], here.tensor_id(here.core))

    def start(self):
        for copy in self.first:
            copy.start()

    def pass_on(self):
        self.first[0].wait_recv()
        self.relay.start()

    def finish(self):
        self.first[1].wait_recv()
        self.relay.wait_recv()
        self.first[0].wait_send()
        self.first[1].wait_send()
        self.relay.wait_send()


class TensorScatter:
    def __init__(self, here, part, from_core, to_across, from_across, send, recv):
        self.here, self.part = here, part
        self.from_core, self.to_across, self.from_across = from_core, to_across, from_across
        core = here.tensor_id(here.core)
        self.far = remote(part.at[here.diagonal], from_core.at[0], send.at[0], recv.at[0], core)
        self.near = remote(part.at[here.core], from_core.at[1], send.at[1], recv.at[1], core)
        self.cross = remote(
            to_across, from_across, send.at[2], recv.at[2], here.tensor_id(here.across)
        )

    def start(self):
        self.far.start()
        self.near.start()

    def pass_on(self):
        self.far.wait_recv()
        total = self.part[self.here.across].astype(F32) + self.from_core[0].astype(F32)
        self.to_across[...] = total.astype(BF16)
        self.cross.start()

    def result(self):
        self.near.wait_recv()
        total = self.part[self.here.t].astype(F32) + self.from_core[1].astype(F32)
        self.cross.wait_recv()
        return total + self.from_across[...].astype(F32)

    def finish(self):
        self.far.wait_send()
        self.near.wait_send()
        self.cross.wait_send()


def scatter_scratch(rows, width):
    return [
        pltpu.VMEM((2, rows, width), BF16),
        pltpu.VMEM((rows, width), BF16),
        pltpu.VMEM((rows, width), BF16),
        pltpu.SemaphoreType.DMA((3,)),
        pltpu.SemaphoreType.DMA((3,)),
    ]


class WeightGather:
    def __init__(self, here, own, out, sz, rz, sx, rx, local):
        self.zs = here.zs
        mine = out.at[here.z, here.x]
        self.keep = pltpu.make_async_copy(own, mine, local)
        self.along = [None] + [
            remote(own, mine, sz.at[k], rz.at[k], here.z_id(k)) for k in range(1, self.zs)
        ]
        self.over = [remote(own, mine, sx.at[0], rx.at[0], here.x_id())]
        for k in range(1, self.zs):
            landed = out.at[here.z_from(k), here.x]
            self.over.append(remote(landed, landed, sx.at[k], rx.at[k], here.x_id()))

    def start(self):
        self.along[1].start()
        self.over[0].start()
        self.keep.start()

    def launch(self, k):
        self.along[k].start()

    def pass_on(self, k):
        self.along[k].wait_recv()
        self.over[k].start()

    def finish(self):
        for copy in self.over:
            copy.wait_recv()
        for copy in self.along[1:] + self.over:
            copy.wait_send()
        self.keep.wait()


def weight_sems(zs):
    return [pltpu.SemaphoreType.DMA((zs,))] * 4 + [pltpu.SemaphoreType.DMA]


class GradScatter:
    def __init__(self, here, part, from_x, to_z, from_z, sz, rz, sx, rx):
        self.here, self.part = here, part
        self.from_x, self.to_z, self.from_z = from_x, to_z, from_z
        self.order = list(range(1, here.zs)) + [0]
        self.over, self.along = {}, {}
        for k in self.order:
            slot = here.z_of(k)
            self.over[k] = remote(
                part.at[slot, 1 - here.x], from_x.at[k], sx.at[k], rx.at[k], here.x_id()
            )
            if k:
                self.along[k] = remote(to_z.at[k], from_z.at[k], sz.at[k], rz.at[k], here.z_id(k))

    def launch(self, k):
        self.over[k].start()

    def half(self, k):
        here = self.here
        self.over[k].wait_recv()
        return self.part[here.z_of(k), here.x].astype(F32) + self.from_x[k].astype(F32)

    def pass_on(self, k):
        self.to_z[k] = self.half(k).astype(BF16)
        self.along[k].start()

    def result(self):
        total = self.half(0)
        for k in range(1, self.here.zs):
            self.along[k].wait_recv()
            total = total + self.from_z[k].astype(F32)
        return total

    def finish(self):
        for k in self.order:
            self.over[k].wait_send()
            if k:
                self.along[k].wait_send()


def grad_scratch(zs, rows, width):
    return [pltpu.VMEM((zs, rows, width), BF16)] * 3 + [pltpu.SemaphoreType.DMA((zs,))] * 4


def tensor_peers(here):
    return [here.tensor_id(t) for t in (here.core, here.across, here.diagonal)]


def dp_peers(here):
    return [here.dp_id(lax.rem(here.d + k, here.dp)) for k in range(1, here.dp)]


def gather_kernel(dp, x_ref, wa_ref, s_ref, x_out, wa_out, s_out, *sems):
    here = Place(dp)
    gx = sems[0:2]
    wa = sems[2:7]
    st_send, st_recv, sd_send, sd_recv, local = sems[7:12]
    greet(tensor_peers(here) + dp_peers(here))
    keeps = [
        pltpu.make_async_copy(x_ref, x_out.at[here.t], local.at[0]),
        pltpu.make_async_copy(s_ref, s_out.at[here.d, here.t], local.at[1]),
    ]
    small = [
        remote(s_ref, s_out.at[here.d, here.t], st_send.at[i], st_recv.at[i], peer)
        for i, peer in enumerate(tensor_peers(here))
    ]
    for copy in small:
        copy.start()
    keeps[1].start()
    a_gather = WeightGather(here, wa_ref, wa_out, *wa)
    a_gather.start()
    x_gather = TensorGather(here, x_ref, x_out, *gx)
    x_gather.start()
    keeps[0].start()
    for copy in small:
        copy.wait_recv()
    keeps[1].wait()
    row = s_out.at[here.d]
    spread = [
        remote(row, row, sd_send.at[k], sd_recv.at[k], here.dp_id(lax.rem(here.d + k, dp)))
        for k in range(1, dp)
    ]
    for copy in spread:
        copy.start()
    for k in range(1, here.zs):
        if k + 1 < here.zs:
            a_gather.launch(k + 1)
        a_gather.pass_on(k)
        if k == 1:
            x_gather.pass_on()
    x_gather.finish()
    a_gather.finish()
    for copy in spread:
        copy.wait_recv()
    for copy in small + spread:
        copy.wait_send()
    keeps[0].wait()


def gather_all(dp, x, wa, small):
    zs = dp // 2
    anywhere = pl.BlockSpec(memory_space=pl.ANY)
    dma = pltpu.SemaphoreType.DMA
    shape = jax.ShapeDtypeStruct
    return pl.pallas_call(
        functools.partial(gather_kernel, dp),
        out_shape=(
            shape((TENSOR,) + x.shape, BF16),
            shape((zs, 2) + wa.shape, BF16),
            shape((dp, TENSOR) + small.shape, BF16),
        ),
        in_specs=[anywhere] * 3,
        out_specs=(anywhere,) * 3,
        scratch_shapes=[dma((3,))] * 2
        + weight_sems(zs)
        + [dma((3,)), dma((3,)), dma((dp,)), dma((dp,)), dma((2,))],
        compiler_params=pltpu.CompilerParams(
            collective_id=0, has_side_effects=True, vmem_limit_bytes=VMEM_LIMIT
        ),
    )(x, wa, small)


LAST = (((1,), (1,)), ((), ()))
FIRST = (((0,), (0,)), ((), ()))


def block_rows(here, j, rows):
    return pl.ds(pl.multiple_of(j * rows, rows), rows)


def middle_kernel(
    dp, qkv, proj_t, x_ref, vec, c_ref, wb_ref,
    middle_out, two_out, mix_out, log_out, c_out, wb_out, part, *rest
):
    here = Place(dp)
    rows = x_ref.shape[0]
    columns = proj_t.shape[1]
    scatter = TensorScatter(here, part, *rest[0:5])
    gather = TensorGather(here, two_out.at[here.t], two_out, *rest[5:7])
    c_gather = TensorGather(here, c_ref, c_out, *rest[7:9])
    b_gather = WeightGather(here, wb_ref, wb_out, *rest[9:14])
    keep = pltpu.make_async_copy(c_ref, c_out.at[here.t], rest[14])

    def attend(j):
        at = block_rows(here, j, rows)
        for h in range(columns // HD):
            low, high = h * HD, (h + 1) * HD
            q = qkv[at, low:high]
            k = qkv[:, columns + low : columns + high]
            v = qkv[:, 2 * columns + low : 2 * columns + high]
            scores = lax.dot_general(q, k, LAST, preferred_element_type=F32) * SCALE
            top = jnp.max(scores, axis=1, keepdims=True)
            exponent = jnp.exp(scores - top)
            total = jnp.sum(exponent, axis=1, keepdims=True)
            probs = (exponent * (1.0 / total)).astype(BF16)
            mix_out[at, low:high] = jnp.dot(probs, v, preferred_element_type=F32).astype(BF16)
            log_out[at, h : h + 1] = top + jnp.log(total)
        part[j] = lax.dot_general(
            mix_out[at, :], proj_t[...], LAST, preferred_element_type=F32
        ).astype(BF16)

    greet(tensor_peers(here) + dp_peers(here))
    b_gather.start()
    attend(here.diagonal)
    scatter.far.start()
    attend(here.core)
    scatter.near.start()
    for k in range(2, here.zs):
        b_gather.launch(k)
    b_gather.pass_on(1)
    attend(here.across)
    scatter.pass_on()
    c_gather.start()
    keep.start()
    attend(here.t)
    middle = x_ref[...].astype(F32) + scatter.result() + vec[3:4]
    middle_out[...] = middle
    two_out[here.t] = layer_norm(middle, vec[1:2], vec[4:5]).astype(BF16)
    gather.start()
    b_gather.pass_on(2)
    c_gather.pass_on()
    gather.pass_on()
    for k in range(3, here.zs):
        b_gather.pass_on(k)
    gather.finish()
    scatter.finish()
    c_gather.finish()
    b_gather.finish()
    keep.wait()


def make_middle(dp, qkv, proj_t, x, vec, cot, wb):
    zs = dp // 2
    vmem = pl.BlockSpec(memory_space=pltpu.VMEM)
    anywhere = pl.BlockSpec(memory_space=pl.ANY)
    rows, width = x.shape
    frames, columns = qkv.shape[0], proj_t.shape[1]
    dma = pltpu.SemaphoreType.DMA
    shape = jax.ShapeDtypeStruct
    return pl.pallas_call(
        functools.partial(middle_kernel, dp),
        out_shape=(
            shape((rows, width), F32),
            shape((TENSOR, rows, width), BF16),
            shape((frames, columns), BF16),
            shape((frames, 128), F32),
            shape((TENSOR, rows, width), BF16),
            shape((zs, 2) + wb.shape, BF16),
        ),
        in_specs=[vmem] * 4 + [anywhere] * 2,
        out_specs=(vmem,) * 4 + (anywhere,) * 2,
        scratch_shapes=[pltpu.VMEM((TENSOR, rows, width), BF16)]
        + scatter_scratch(rows, width)
        + [dma((3,))] * 4
        + weight_sems(zs)
        + [dma],
        compiler_params=pltpu.CompilerParams(
            collective_id=1, has_side_effects=True, vmem_limit_bytes=VMEM_LIMIT
        ),
    )(qkv, proj_t, x, vec, cot, wb)


def weight_grad(left, right, slots, share, first, tiles):
    width = slots.shape[0] * 2 * share
    tall = width // tiles
    for i in range(tiles):
        piece = left(i * tall, (i + 1) * tall)
        product = lax.dot_general(piece, right, FIRST, preferred_element_type=F32).astype(BF16)
        for n in range(tall // share):
            slot = i * (tall // share) + n
            slots[slot // 2, slot % 2, 0:share, first : first + right.shape[1]] = product[
                n * share : (n + 1) * share
            ]


def back_kernel(
    dp, share, grad_part, feed_part, middle, x_ref, cot, vec, qkv, wa, log, two, hid, act, cots, normed,
    attended, up_row, out, in_out, ga_out, gb_out, sum_out,
    mgrad_out, attn_out, grads, ga, gb, part, dk_sum, dv_sum, near, around, *rest
):
    here = Place(dp)
    rows = cot.shape[0]
    frames = qkv.shape[0]
    columns = qkv.shape[1] // 3
    heads = columns // HD
    hidden_width = hid.shape[1]
    proj = slice(3 * columns, 4 * columns)
    grad_scatter = TensorScatter(here, grad_part, *rest[0:5])
    feed_scatter = TensorScatter(here, feed_part, *rest[5:10])
    norm_scatter = TensorScatter(here, part, *rest[10:15])
    gather = TensorGather(here, attn_out.at[here.t], attn_out, *rest[15:17])
    b_scatter = GradScatter(here, gb, *rest[17:24])
    a_scatter = GradScatter(here, ga, *rest[24:31])
    st_send, st_recv, sd_send, sd_recv = rest[31:35]

    def stacked_columns(ref):
        return lambda low, high: ref[:, :, low:high].reshape(frames, high - low)

    def attend_back(j, first):
        at = block_rows(here, j, rows)
        mixed = jnp.dot(attn_out[j], wa[:, proj], preferred_element_type=F32).astype(BF16)
        for h in range(heads):
            low, high = h * HD, (h + 1) * HD
            g = mixed[:, low:high]
            q = qkv[at, low:high]
            k = qkv[:, columns + low : columns + high]
            v = qkv[:, 2 * columns + low : 2 * columns + high]
            scores = lax.dot_general(q, k, LAST, preferred_element_type=F32) * SCALE
            probs = jnp.exp(scores - log[at, h : h + 1])
            prob_grad = lax.dot_general(g, v, LAST, preferred_element_type=F32)
            row_dot = jnp.sum(probs * prob_grad, axis=1, keepdims=True)
            score_grad = (probs * (prob_grad - row_dot)).astype(BF16)
            grads[at, low:high] = (
                jnp.dot(score_grad, k, preferred_element_type=F32) * SCALE
            ).astype(BF16)
            dk = lax.dot_general(score_grad, q, FIRST, preferred_element_type=F32)
            dv = lax.dot_general(probs.astype(BF16), g, FIRST, preferred_element_type=F32)
            if first:
                dk_sum[h] = dk
                dv_sum[h] = dv
            else:
                dk_sum[h] += dk
                dv_sum[h] += dv

    def normed_part(j):
        part[j] = lax.dot_general(
            grads[block_rows(here, j, rows), :], wa[:, : 3 * columns], LAST,
            preferred_element_type=F32,
        ).astype(BF16)

    greet(tensor_peers(here) + dp_peers(here))
    grad_scatter.start()
    weight_grad(stacked_columns(two), hid[...], gb, share, 0, 2)
    grad_scatter.pass_on()
    weight_grad(stacked_columns(cots), act[...], gb, share, hidden_width, 2)
    b_scatter.launch(1)
    b_scatter.launch(2)
    feed_scatter.start()
    incoming = grad_scatter.result()
    mid = middle[...]
    mid_part, gain_sum, shift_sum = norm_back(mid, vec[1:2], incoming)
    grad_out = cot[...].astype(F32)
    mgrad = grad_out + mid_part
    attn_out[here.t] = mgrad.astype(BF16)
    gather.start()
    for k in range(3, here.zs):
        b_scatter.launch(k)
    b_scatter.launch(0)
    mgrad_out[...] = mgrad
    near[0, 1:2] = gain_sum
    near[0, 3:4] = jnp.sum(mgrad, axis=0, keepdims=True)
    near[0, 4:5] = shift_sum
    near[0, 5:6] = jnp.sum(grad_out, axis=0, keepdims=True)
    near[0, 6:8] = jnp.zeros((2, near.shape[2]), F32)
    attend_back(here.t, True)
    b_scatter.pass_on(1)
    gather.pass_on()
    feed_scatter.pass_on()
    gather.first[1].wait_recv()
    attend_back(here.core, False)
    b_scatter.pass_on(2)
    attend_back(here.across, False)
    gather.relay.wait_recv()
    attend_back(here.diagonal, False)
    for h in range(heads):
        low, high = h * HD, (h + 1) * HD
        grads[:, columns + low : columns + high] = (dk_sum[h] * SCALE).astype(BF16)
        grads[:, 2 * columns + low : 2 * columns + high] = dv_sum[h].astype(BF16)
    normed_part(here.diagonal)
    norm_scatter.far.start()
    normed_part(here.core)
    norm_scatter.near.start()
    for k in range(3, here.zs):
        b_scatter.pass_on(k)
    weight_grad(lambda low, high: normed[:, low:high], grads[...], ga, share, 0, 2)
    weight_grad(stacked_columns(attn_out), attended[...], ga, share, 3 * columns, 2)
    a_scatter.launch(1)
    a_scatter.launch(2)
    normed_part(here.across)
    norm_scatter.pass_on()
    normed_part(here.t)
    for k in range(3, here.zs):
        a_scatter.launch(k)
    a_scatter.launch(0)
    a_scatter.pass_on(1)
    in_part, gain_sum, shift_sum = norm_back(
        x_ref[...].astype(F32), vec[0:1], norm_scatter.result()
    )
    near[0, 0:1] = gain_sum
    near[0, 2:3] = shift_sum
    small = [
        remote(near.at[0], near.at[i + 1], st_send.at[i], st_recv.at[i], peer)
        for i, peer in enumerate(tensor_peers(here))
    ]
    for copy in small:
        copy.start()
    in_out[...] = mgrad_out[...] + in_part
    a_scatter.pass_on(2)
    for copy in small:
        copy.wait_recv()
    around[0, 0:8] = (near[0] + near[1]) + (near[2] + near[3])
    around[0, 8:16] = jnp.zeros((8, around.shape[2]), F32)
    around[0, 8:9, :hidden_width] = up_row[...]
    around[0, 9:10, :columns] = jnp.sum(grads[:, :columns].astype(F32), axis=0, keepdims=True)
    around[0, 10:11, :columns] = jnp.sum(
        grads[:, 2 * columns :].astype(F32), axis=0, keepdims=True
    )
    spread = [
        remote(
            around.at[0], around.at[k], sd_send.at[k], sd_recv.at[k],
            here.dp_id(lax.rem(here.d + k, dp)),
        )
        for k in range(1, dp)
    ]
    for copy in spread:
        copy.start()
    for k in range(3, here.zs):
        a_scatter.pass_on(k)
    out[...] = (mid + feed_scatter.result() + vec[5:6]).astype(BF16)
    gb_out[...] = b_scatter.result()
    total = around[0]
    for k in range(1, dp):
        spread[k - 1].wait_recv()
        total = total + around[k]
    sum_out[...] = total
    ga_out[...] = a_scatter.result()
    for copy in gather.first + [gather.relay] + small + spread:
        copy.wait_send()
    for scatter in (grad_scatter, feed_scatter, norm_scatter, a_scatter, b_scatter):
        scatter.finish()


def go_back(dp, share, padded, *args):
    cot, qkv, hid = args[4], args[6], args[10]
    zs = dp // 2
    vmem = pl.BlockSpec(memory_space=pltpu.VMEM)
    rows, width = cot.shape
    frames = qkv.shape[0]
    columns = qkv.shape[1] // 3
    wide_a, wide_b = 4 * columns, 2 * hid.shape[1]
    dma = pltpu.SemaphoreType.DMA
    shape = jax.ShapeDtypeStruct
    return pl.pallas_call(
        functools.partial(back_kernel, dp, share),
        out_shape=(
            shape((rows, width), BF16),
            shape((rows, width), F32),
            shape((padded, wide_a), F32),
            shape((padded, wide_b), F32),
            shape((16, width), F32),
        ),
        in_specs=[vmem] * len(args),
        out_specs=(vmem,) * 5,
        scratch_shapes=[
            pltpu.VMEM((rows, width), F32),
            pltpu.VMEM((TENSOR, rows, width), BF16),
            pltpu.VMEM(qkv.shape, BF16),
            pltpu.VMEM((zs, 2, padded, wide_a), BF16),
            pltpu.VMEM((zs, 2, padded, wide_b), BF16),
            pltpu.VMEM((TENSOR, rows, width), BF16),
        ]
        + [pltpu.VMEM((columns // HD, frames, HD), F32)] * 2
        + [pltpu.VMEM((TENSOR, 8, width), F32), pltpu.VMEM((dp, 16, width), F32)]
        + scatter_scratch(rows, width) * 3
        + [dma((3,)), dma((3,))]
        + grad_scratch(zs, padded, wide_b)
        + grad_scratch(zs, padded, wide_a)
        + [dma((3,)), dma((3,)), dma((dp,)), dma((dp,))],
        compiler_params=pltpu.CompilerParams(
            collective_id=2, has_side_effects=True, vmem_limit_bytes=VMEM_LIMIT
        ),
    )(*args)


def pad_rows(array, rows, axis):
    extra = rows - array.shape[axis]
    if extra == 0:
        return array
    widths = [(0, 0)] * array.ndim
    widths[axis] = (0, extra)
    return jnp.pad(array, widths)


def body(dp, inputs, cotangent, qkv_weight, proj_weight, up_weight, down_weight, qv_bias, up_bias, norm_gains, row_biases):
    zs = dp // 2
    rows, width = inputs.shape
    share = qkv_weight.shape[1]
    padded = -(-share // 16) * 16
    columns = qkv_weight.shape[2]
    hidden_width = up_weight.shape[1]
    heads = columns // HD
    frames = rows * TENSOR

    def wide(array):
        array = array.reshape(array.shape[0], -1)
        return jnp.pad(array, ((0, 0), (0, 128 - array.shape[1])))

    wa = jnp.concatenate([qkv_weight[0], qkv_weight[1], qkv_weight[2], proj_weight.T], axis=1)
    wb = jnp.concatenate([up_weight, down_weight.T], axis=1)
    bit = norm_gains.shape[1]
    small = jnp.concatenate(
        [wide(norm_gains), wide(row_biases), wide(qv_bias), wide(up_bias[None])], axis=0
    )
    small = pad_rows(small, 16, 0)
    x_all, wa_all, small_all = gather_all(dp, inputs, pad_rows(wa, padded, 0), small)

    def whole(array):
        return array[:, :, :share].reshape(width, array.shape[3])

    x_all = x_all.reshape(frames, width)
    wa_all = whole(wa_all)
    qkv_full, proj_t = wa_all[:, : 3 * columns], wa_all[:, 3 * columns :]
    small_all = small_all.astype(F32)
    tensor = lax.axis_index("tensor")
    vec = small_all[:, :, 0:8, :bit].transpose(2, 0, 1, 3).reshape(8, width)
    mine = lax.dynamic_index_in_dim(small_all, tensor, 1, keepdims=False)
    bits = qv_bias.shape[1]
    qv_full = mine[:, 6:8, :bits].transpose(1, 0, 2).reshape(2, columns)
    up_bias_full = mine[:, 8, : up_bias.shape[0]].reshape(hidden_width)

    normed = layer_norm(x_all.astype(F32), vec[0:1], vec[2:3]).astype(BF16)
    bias_row = jnp.concatenate([qv_full[0], jnp.zeros_like(qv_full[0]), qv_full[1]])
    projected = (jnp.dot(normed, qkv_full, preferred_element_type=F32) + bias_row).astype(BF16)

    def blocks(array):
        return array.reshape(TENSOR, rows, width)

    middle, normed_two, attended, logsum, cot_all, wb_all = make_middle(
        dp, projected, proj_t, inputs, vec, cotangent, pad_rows(wb, padded, 0)
    )
    normed_two = normed_two.reshape(frames, width)
    cot_all = cot_all.reshape(frames, width)
    wb_all = whole(wb_all)
    up_full, down_t = wb_all[:, :hidden_width], wb_all[:, hidden_width:]
    hidden = jnp.dot(normed_two, up_full, preferred_element_type=F32) + up_bias_full
    cumulative = 0.5 * (1.0 + jax.scipy.special.erf(hidden * ROOT_HALF))
    activated = (hidden * cumulative).astype(BF16)
    slope = cumulative + hidden * jnp.exp(-0.5 * hidden * hidden) * ROOT_TWO_PI_INVERSE
    act_grad = jnp.dot(cot_all, down_t, preferred_element_type=F32)
    hidden_grad = (act_grad * slope).astype(BF16)
    grad_part = lax.dot_general(hidden_grad, up_full, LAST, preferred_element_type=F32)
    feed_part = lax.dot_general(activated, down_t, LAST, preferred_element_type=F32)
    up_bias_grad = jnp.sum(hidden_grad.astype(F32), axis=0, keepdims=True)
    outputs, input_grad, ga_out, gb_out, all_sums = go_back(
        dp, share, padded,
        blocks(grad_part.astype(BF16)), blocks(feed_part.astype(BF16)), middle, inputs, cotangent, vec,
        projected, wa_all, logsum, blocks(normed_two), hidden_grad, activated, blocks(cot_all), normed,
        attended, up_bias_grad,
    )
    ga_out, gb_out = ga_out[:share], gb_out[:share]
    place = lax.axis_index("dp")
    both = place * TENSOR + tensor
    qkv_grad_out = ga_out[:, : 3 * columns].reshape(share, 3, columns).transpose(1, 0, 2)
    vectors = lax.dynamic_slice(all_sums, (0, both * bit), (6, bit))
    qv_out = lax.dynamic_slice(all_sums, (9, place * bits), (2, bits))
    up_bits = up_bias.shape[0]
    up_bias_out = lax.dynamic_slice(all_sums, (8, place * up_bits), (1, up_bits))[0]
    return (
        outputs,
        input_grad,
        qkv_grad_out,
        ga_out[:, 3 * columns :].T,
        gb_out[:, :hidden_width],
        gb_out[:, hidden_width:].T,
        qv_out,
        up_bias_out,
        vectors[0:2],
        vectors[2:6],
    )


def solution(mesh):
    both = ("dp", "tensor")
    placed = (
        P(both, None),
        P(both, None),
        P(None, "dp", "tensor"),
        P("tensor", "dp"),
        P("dp", "tensor"),
        P("tensor", "dp"),
        P(None, ("tensor", "dp")),
        P(("tensor", "dp")),
        P(None, both),
        P(None, both),
    )
    return jax.shard_map(
        functools.partial(body, mesh.shape["dp"]),
        mesh=mesh,
        in_specs=placed,
        out_specs=(
            P(both, None),
            P(both, None),
            P(None, "dp", "tensor"),
            P("tensor", "dp"),
            P("dp", "tensor"),
            P("tensor", "dp"),
            P(None, ("tensor", "dp")),
            P(("tensor", "dp")),
            P(None, both),
            P(None, both),
        ),
        check_vma=False,
    )
```

```python
import functools

import jax
import jax.numpy as jnp
from jax import lax
from jax.experimental import pallas as pl
from jax.experimental.pallas import tpu as pltpu
from jax.sharding import PartitionSpec as P

HD = 64
EPSILON = 1e-05
SCALE = 0.125
ROOT_HALF = 0.7071067811865476
ROOT_TWO_PI_INVERSE = 0.3989422804014327
F32 = jnp.float32
BF16 = jnp.bfloat16
VMEM_LIMIT = 50 * 1024 * 1024
MESH = pl.DeviceIdType.MESH
TENSOR = 4


def layer_norm(values, gain_row, shift_row):
    center = values - jnp.mean(values, axis=-1, keepdims=True)
    spread = jnp.mean(center * center, axis=-1, keepdims=True)
    return center * lax.rsqrt(spread + EPSILON) * gain_row + shift_row


def norm_back(values, gain_row, incoming):
    center = values - jnp.mean(values, axis=-1, keepdims=True)
    spread = jnp.mean(center * center, axis=-1, keepdims=True)
    inverse = lax.rsqrt(spread + EPSILON)
    unit_rows = center * inverse
    scaled = incoming * gain_row
    grad_in = inverse * (
        scaled
        - jnp.mean(scaled, axis=-1, keepdims=True)
        - unit_rows * jnp.mean(scaled * unit_rows, axis=-1, keepdims=True)
    )
    return (
        grad_in,
        jnp.sum(incoming * unit_rows, axis=0, keepdims=True),
        jnp.sum(incoming, axis=0, keepdims=True),
    )


class Place:
    def __init__(self, dp):
        self.dp = dp
        self.zs = dp // 2
        self.d = lax.axis_index("dp")
        self.t = lax.axis_index("tensor")
        self.z = self.d // 2
        self.x = lax.rem(self.d, 2)
        self.core = self.t + 1 - 2 * lax.rem(self.t, 2)
        self.across = lax.rem(self.t + 2, TENSOR)
        self.diagonal = lax.rem(self.core + 2, TENSOR)

    def tensor_id(self, t):
        return {"dp": self.d, "tensor": t}

    def dp_id(self, d):
        return {"dp": d, "tensor": self.t}

    def x_id(self):
        return self.dp_id(self.z * 2 + 1 - self.x)

    def z_of(self, k):
        return lax.rem(self.z + k, self.zs)

    def z_from(self, k):
        return lax.rem(self.z + self.zs - k, self.zs)

    def z_id(self, k):
        return self.dp_id(self.z_of(k) * 2 + self.x)


def greet(peers):
    barrier = pltpu.get_barrier_semaphore()
    for peer in peers:
        pl.semaphore_signal(barrier, inc=1, device_id=peer, device_id_type=MESH)
    pl.semaphore_wait(barrier, len(peers))


def remote(src, dst, send, recv, peer):
    return pltpu.make_async_remote_copy(
        src_ref=src, dst_ref=dst, send_sem=send, recv_sem=recv, device_id=peer, device_id_type=MESH
    )


class TensorGather:
    def __init__(self, here, own, out, send, recv):
        t = here.t
        self.first = [
            remote(own, out.at[t], send.at[0], recv.at[0], here.tensor_id(here.across)),
            remote(own, out.at[t], send.at[1], recv.at[1], here.tensor_id(here.core)),
        ]
        landed = out.at[here.across]
        self.relay = remote(landed, landed, send.at[2], recv.at[2], here.tensor_id(here.core))

    def start(self):
        for copy in self.first:
            copy.start()

    def pass_on(self):
        self.first[0].wait_recv()
        self.relay.start()

    def finish(self):
        self.first[1].wait_recv()
        self.relay.wait_recv()
        self.first[0].wait_send()
        self.first[1].wait_send()
        self.relay.wait_send()


class TensorScatter:
    def __init__(self, here, part, from_core, to_across, from_across, send, recv):
        self.here, self.part = here, part
        self.from_core, self.to_across, self.from_across = from_core, to_across, from_across
        core = here.tensor_id(here.core)
        self.far = remote(part.at[here.diagonal], from_core.at[0], send.at[0], recv.at[0], core)
        self.near = remote(part.at[here.core], from_core.at[1], send.at[1], recv.at[1], core)
        self.cross = remote(
            to_across, from_across, send.at[2], recv.at[2], here.tensor_id(here.across)
        )

    def start(self):
        self.far.start()
        self.near.start()

    def pass_on(self):
        self.far.wait_recv()
        total = self.part[self.here.across].astype(F32) + self.from_core[0].astype(F32)
        self.to_across[...] = total.astype(BF16)
        self.cross.start()

    def result(self):
        self.near.wait_recv()
        total = self.part[self.here.t].astype(F32) + self.from_core[1].astype(F32)
        self.cross.wait_recv()
        return total + self.from_across[...].astype(F32)

    def finish(self):
        self.far.wait_send()
        self.near.wait_send()
        self.cross.wait_send()


def scatter_scratch(rows, width):
    return [
        pltpu.VMEM((2, rows, width), BF16),
        pltpu.VMEM((rows, width), BF16),
        pltpu.VMEM((rows, width), BF16),
        pltpu.SemaphoreType.DMA((3,)),
        pltpu.SemaphoreType.DMA((3,)),
    ]


class WeightGather:
    def __init__(self, here, own, out, sz, rz, sx, rx, local):
        self.zs = here.zs
        mine = out.at[here.z, here.x]
        self.keep = pltpu.make_async_copy(own, mine, local)
        self.along = [None] + [
            remote(own, mine, sz.at[k], rz.at[k], here.z_id(k)) for k in range(1, self.zs)
        ]
        self.over = [remote(own, mine, sx.at[0], rx.at[0], here.x_id())]
        for k in range(1, self.zs):
            landed = out.at[here.z_from(k), here.x]
            self.over.append(remote(landed, landed, sx.at[k], rx.at[k], here.x_id()))

    def start(self):
        self.along[1].start()
        self.over[0].start()
        self.keep.start()

    def launch(self, k):
        self.along[k].start()

    def pass_on(self, k):
        self.along[k].wait_recv()
        self.over[k].start()

    def finish(self):
        for copy in self.over:
            copy.wait_recv()
        for copy in self.along[1:] + self.over:
            copy.wait_send()
        self.keep.wait()


def weight_sems(zs):
    return [pltpu.SemaphoreType.DMA((zs,))] * 4 + [pltpu.SemaphoreType.DMA]


class GradScatter:
    def __init__(self, here, part, from_x, to_z, from_z, sz, rz, sx, rx):
        self.here, self.part = here, part
        self.from_x, self.to_z, self.from_z = from_x, to_z, from_z
        self.order = list(range(1, here.zs)) + [0]
        self.over, self.along = {}, {}
        for k in self.order:
            slot = here.z_of(k)
            self.over[k] = remote(
                part.at[slot, 1 - here.x], from_x.at[k], sx.at[k], rx.at[k], here.x_id()
            )
            if k:
                self.along[k] = remote(to_z.at[k], from_z.at[k], sz.at[k], rz.at[k], here.z_id(k))

    def launch(self, k):
        self.over[k].start()

    def half(self, k):
        here = self.here
        self.over[k].wait_recv()
        return self.part[here.z_of(k), here.x].astype(F32) + self.from_x[k].astype(F32)

    def pass_on(self, k):
        self.to_z[k] = self.half(k).astype(BF16)
        self.along[k].start()

    def result(self):
        total = self.half(0)
        for k in range(1, self.here.zs):
            self.along[k].wait_recv()
            total = total + self.from_z[k].astype(F32)
        return total

    def finish(self):
        for k in self.order:
            self.over[k].wait_send()
            if k:
                self.along[k].wait_send()


def grad_scratch(zs, rows, width):
    return [pltpu.VMEM((zs, rows, width), BF16)] * 3 + [pltpu.SemaphoreType.DMA((zs,))] * 4


def tensor_peers(here):
    return [here.tensor_id(t) for t in (here.core, here.across, here.diagonal)]


def dp_peers(here):
    return [here.dp_id(lax.rem(here.d + k, here.dp)) for k in range(1, here.dp)]


def gather_kernel(dp, x_ref, wa_ref, s_ref, x_out, wa_out, s_out, *sems):
    here = Place(dp)
    gx = sems[0:2]
    wa = sems[2:7]
    st_send, st_recv, sd_send, sd_recv, local = sems[7:12]
    greet(tensor_peers(here) + dp_peers(here))
    keeps = [
        pltpu.make_async_copy(x_ref, x_out.at[here.t], local.at[0]),
        pltpu.make_async_copy(s_ref, s_out.at[here.d, here.t], local.at[1]),
    ]
    small = [
        remote(s_ref, s_out.at[here.d, here.t], st_send.at[i], st_recv.at[i], peer)
        for i, peer in enumerate(tensor_peers(here))
    ]
    for copy in small:
        copy.start()
    keeps[1].start()
    a_gather = WeightGather(here, wa_ref, wa_out, *wa)
    a_gather.start()
    for k in range(2, here.zs):
        a_gather.launch(k)
    x_gather = TensorGather(here, x_ref, x_out, *gx)
    x_gather.start()
    keeps[0].start()
    for copy in small:
        copy.wait_recv()
    keeps[1].wait()
    row = s_out.at[here.d]
    spread = [
        remote(row, row, sd_send.at[k], sd_recv.at[k], here.dp_id(lax.rem(here.d + k, dp)))
        for k in range(1, dp)
    ]
    for copy in spread:
        copy.start()
    for k in range(1, here.zs):
        a_gather.pass_on(k)
        if k == 1:
            x_gather.pass_on()
    x_gather.finish()
    a_gather.finish()
    for copy in spread:
        copy.wait_recv()
    for copy in small + spread:
        copy.wait_send()
    keeps[0].wait()


def gather_all(dp, x, wa, small):
    zs = dp // 2
    anywhere = pl.BlockSpec(memory_space=pl.ANY)
    dma = pltpu.SemaphoreType.DMA
    shape = jax.ShapeDtypeStruct
    return pl.pallas_call(
        functools.partial(gather_kernel, dp),
        out_shape=(
            shape((TENSOR,) + x.shape, BF16),
            shape((zs, 2) + wa.shape, BF16),
            shape((dp, TENSOR) + small.shape, BF16),
        ),
        in_specs=[anywhere] * 3,
        out_specs=(anywhere,) * 3,
        scratch_shapes=[dma((3,))] * 2
        + weight_sems(zs)
        + [dma((3,)), dma((3,)), dma((dp,)), dma((dp,)), dma((2,))],
        compiler_params=pltpu.CompilerParams(
            collective_id=0, has_side_effects=True, vmem_limit_bytes=VMEM_LIMIT
        ),
    )(x, wa, small)


LAST = (((1,), (1,)), ((), ()))
FIRST = (((0,), (0,)), ((), ()))


def block_rows(here, j, rows):
    return pl.ds(pl.multiple_of(j * rows, rows), rows)


def middle_kernel(
    dp, qkv, proj_t, x_ref, vec, c_ref, wb_ref,
    middle_out, two_out, mix_out, log_out, c_out, wb_out, part, *rest
):
    here = Place(dp)
    rows = x_ref.shape[0]
    columns = proj_t.shape[1]
    scatter = TensorScatter(here, part, *rest[0:5])
    gather = TensorGather(here, two_out.at[here.t], two_out, *rest[5:7])
    c_gather = TensorGather(here, c_ref, c_out, *rest[7:9])
    b_gather = WeightGather(here, wb_ref, wb_out, *rest[9:14])
    keep = pltpu.make_async_copy(c_ref, c_out.at[here.t], rest[14])

    def attend(j):
        at = block_rows(here, j, rows)
        for h in range(columns // HD):
            low, high = h * HD, (h + 1) * HD
            q = qkv[at, low:high]
            k = qkv[:, columns + low : columns + high]
            v = qkv[:, 2 * columns + low : 2 * columns + high]
            scores = lax.dot_general(q, k, LAST, preferred_element_type=F32) * SCALE
            top = jnp.max(scores, axis=1, keepdims=True)
            exponent = jnp.exp(scores - top)
            total = jnp.sum(exponent, axis=1, keepdims=True)
            probs = (exponent * (1.0 / total)).astype(BF16)
            mix_out[at, low:high] = jnp.dot(probs, v, preferred_element_type=F32).astype(BF16)
            log_out[at, h : h + 1] = top + jnp.log(total)
        part[j] = lax.dot_general(
            mix_out[at, :], proj_t[...], LAST, preferred_element_type=F32
        ).astype(BF16)

    greet(tensor_peers(here) + dp_peers(here))
    b_gather.start()
    for k in range(2, here.zs):
        b_gather.launch(k)
    attend(here.diagonal)
    scatter.far.start()
    attend(here.core)
    scatter.near.start()
    attend(here.across)
    scatter.pass_on()
    b_gather.pass_on(1)
    c_gather.start()
    keep.start()
    attend(here.t)
    middle = x_ref[...].astype(F32) + scatter.result() + vec[3:4]
    middle_out[...] = middle
    two_out[here.t] = layer_norm(middle, vec[1:2], vec[4:5]).astype(BF16)
    gather.start()
    b_gather.pass_on(2)
    c_gather.pass_on()
    gather.pass_on()
    for k in range(3, here.zs):
        b_gather.pass_on(k)
    gather.finish()
    scatter.finish()
    c_gather.finish()
    b_gather.finish()
    keep.wait()


def make_middle(dp, qkv, proj_t, x, vec, cot, wb):
    zs = dp // 2
    vmem = pl.BlockSpec(memory_space=pltpu.VMEM)
    anywhere = pl.BlockSpec(memory_space=pl.ANY)
    rows, width = x.shape
    frames, columns = qkv.shape[0], proj_t.shape[1]
    dma = pltpu.SemaphoreType.DMA
    shape = jax.ShapeDtypeStruct
    return pl.pallas_call(
        functools.partial(middle_kernel, dp),
        out_shape=(
            shape((rows, width), F32),
            shape((TENSOR, rows, width), BF16),
            shape((frames, columns), BF16),
            shape((frames, 128), F32),
            shape((TENSOR, rows, width), BF16),
            shape((zs, 2) + wb.shape, BF16),
        ),
        in_specs=[vmem] * 4 + [anywhere] * 2,
        out_specs=(vmem,) * 4 + (anywhere,) * 2,
        scratch_shapes=[pltpu.VMEM((TENSOR, rows, width), BF16)]
        + scatter_scratch(rows, width)
        + [dma((3,))] * 4
        + weight_sems(zs)
        + [dma],
        compiler_params=pltpu.CompilerParams(
            collective_id=1, has_side_effects=True, vmem_limit_bytes=VMEM_LIMIT
        ),
    )(qkv, proj_t, x, vec, cot, wb)


def weight_grad(left, right, slots, share, first, tiles):
    width = slots.shape[0] * 2 * share
    tall = width // tiles
    for i in range(tiles):
        piece = left(i * tall, (i + 1) * tall)
        product = lax.dot_general(piece, right, FIRST, preferred_element_type=F32).astype(BF16)
        for n in range(tall // share):
            slot = i * (tall // share) + n
            slots[slot // 2, slot % 2, 0:share, first : first + right.shape[1]] = product[
                n * share : (n + 1) * share
            ]


def back_kernel(
    dp, share, grad_part, feed_part, middle, x_ref, cot, vec, qkv, wa, log, two, hid, act, cots, normed,
    attended, up_row, out, in_out, ga_out, gb_out, sum_out,
    mgrad_out, attn_out, grads, ga, gb, part, dk_sum, dv_sum, near, around, *rest
):
    here = Place(dp)
    rows = cot.shape[0]
    frames = qkv.shape[0]
    columns = qkv.shape[1] // 3
    heads = columns // HD
    hidden_width = hid.shape[1]
    proj = slice(3 * columns, 4 * columns)
    grad_scatter = TensorScatter(here, grad_part, *rest[0:5])
    feed_scatter = TensorScatter(here, feed_part, *rest[5:10])
    norm_scatter = TensorScatter(here, part, *rest[10:15])
    gather = TensorGather(here, attn_out.at[here.t], attn_out, *rest[15:17])
    b_scatter = GradScatter(here, gb, *rest[17:24])
    a_scatter = GradScatter(here, ga, *rest[24:31])
    st_send, st_recv, sd_send, sd_recv = rest[31:35]

    def stacked_columns(ref):
        return lambda low, high: ref[:, :, low:high].reshape(frames, high - low)

    def attend_back(j, first):
        at = block_rows(here, j, rows)
        mixed = jnp.dot(attn_out[j], wa[:, proj], preferred_element_type=F32).astype(BF16)
        for h in range(heads):
            low, high = h * HD, (h + 1) * HD
            g = mixed[:, low:high]
            q = qkv[at, low:high]
            k = qkv[:, columns + low : columns + high]
            v = qkv[:, 2 * columns + low : 2 * columns + high]
            scores = lax.dot_general(q, k, LAST, preferred_element_type=F32) * SCALE
            probs = jnp.exp(scores - log[at, h : h + 1])
            prob_grad = lax.dot_general(g, v, LAST, preferred_element_type=F32)
            row_dot = jnp.sum(probs * prob_grad, axis=1, keepdims=True)
            score_grad = (probs * (prob_grad - row_dot)).astype(BF16)
            grads[at, low:high] = (
                jnp.dot(score_grad, k, preferred_element_type=F32) * SCALE
            ).astype(BF16)
            dk = lax.dot_general(score_grad, q, FIRST, preferred_element_type=F32)
            dv = lax.dot_general(probs.astype(BF16), g, FIRST, preferred_element_type=F32)
            if first:
                dk_sum[h] = dk
                dv_sum[h] = dv
            else:
                dk_sum[h] += dk
                dv_sum[h] += dv

    def normed_part(j):
        part[j] = lax.dot_general(
            grads[block_rows(here, j, rows), :], wa[:, : 3 * columns], LAST,
            preferred_element_type=F32,
        ).astype(BF16)

    greet(tensor_peers(here) + dp_peers(here))
    grad_scatter.start()
    weight_grad(stacked_columns(two), hid[...], gb, share, 0, 2)
    grad_scatter.pass_on()
    weight_grad(stacked_columns(cots), act[...], gb, share, hidden_width, 2)
    b_scatter.launch(1)
    b_scatter.launch(2)
    feed_scatter.start()
    incoming = grad_scatter.result()
    mid = middle[...]
    mid_part, gain_sum, shift_sum = norm_back(mid, vec[1:2], incoming)
    grad_out = cot[...].astype(F32)
    mgrad = grad_out + mid_part
    attn_out[here.t] = mgrad.astype(BF16)
    gather.start()
    for k in range(3, here.zs):
        b_scatter.launch(k)
    b_scatter.launch(0)
    mgrad_out[...] = mgrad
    near[0, 1:2] = gain_sum
    near[0, 3:4] = jnp.sum(mgrad, axis=0, keepdims=True)
    near[0, 4:5] = shift_sum
    near[0, 5:6] = jnp.sum(grad_out, axis=0, keepdims=True)
    near[0, 6:8] = jnp.zeros((2, near.shape[2]), F32)
    attend_back(here.t, True)
    b_scatter.pass_on(1)
    gather.pass_on()
    feed_scatter.pass_on()
    gather.first[1].wait_recv()
    attend_back(here.core, False)
    b_scatter.pass_on(2)
    attend_back(here.across, False)
    gather.relay.wait_recv()
    attend_back(here.diagonal, False)
    for h in range(heads):
        low, high = h * HD, (h + 1) * HD
        grads[:, columns + low : columns + high] = (dk_sum[h] * SCALE).astype(BF16)
        grads[:, 2 * columns + low : 2 * columns + high] = dv_sum[h].astype(BF16)
    normed_part(here.diagonal)
    norm_scatter.far.start()
    normed_part(here.core)
    norm_scatter.near.start()
    for k in range(3, here.zs):
        b_scatter.pass_on(k)
    weight_grad(lambda low, high: normed[:, low:high], grads[...], ga, share, 0, 2)
    weight_grad(stacked_columns(attn_out), attended[...], ga, share, 3 * columns, 2)
    a_scatter.launch(1)
    a_scatter.launch(2)
    normed_part(here.across)
    norm_scatter.pass_on()
    normed_part(here.t)
    for k in range(3, here.zs):
        a_scatter.launch(k)
    a_scatter.launch(0)
    a_scatter.pass_on(1)
    in_part, gain_sum, shift_sum = norm_back(
        x_ref[...].astype(F32), vec[0:1], norm_scatter.result()
    )
    near[0, 0:1] = gain_sum
    near[0, 2:3] = shift_sum
    small = [
        remote(near.at[0], near.at[i + 1], st_send.at[i], st_recv.at[i], peer)
        for i, peer in enumerate(tensor_peers(here))
    ]
    for copy in small:
        copy.start()
    in_out[...] = mgrad_out[...] + in_part
    a_scatter.pass_on(2)
    for copy in small:
        copy.wait_recv()
    around[0, 0:8] = (near[0] + near[1]) + (near[2] + near[3])
    around[0, 8:16] = jnp.zeros((8, around.shape[2]), F32)
    around[0, 8:9, :hidden_width] = up_row[...]
    around[0, 9:10, :columns] = jnp.sum(grads[:, :columns].astype(F32), axis=0, keepdims=True)
    around[0, 10:11, :columns] = jnp.sum(
        grads[:, 2 * columns :].astype(F32), axis=0, keepdims=True
    )
    spread = [
        remote(
            around.at[0], around.at[k], sd_send.at[k], sd_recv.at[k],
            here.dp_id(lax.rem(here.d + k, dp)),
        )
        for k in range(1, dp)
    ]
    for copy in spread:
        copy.start()
    for k in range(3, here.zs):
        a_scatter.pass_on(k)
    out[...] = (mid + feed_scatter.result() + vec[5:6]).astype(BF16)
    gb_out[...] = b_scatter.result()
    total = around[0]
    for k in range(1, dp):
        spread[k - 1].wait_recv()
        total = total + around[k]
    sum_out[...] = total
    ga_out[...] = a_scatter.result()
    for copy in gather.first + [gather.relay] + small + spread:
        copy.wait_send()
    for scatter in (grad_scatter, feed_scatter, norm_scatter, a_scatter, b_scatter):
        scatter.finish()


def go_back(dp, share, padded, *args):
    cot, qkv, hid = args[4], args[6], args[10]
    zs = dp // 2
    vmem = pl.BlockSpec(memory_space=pltpu.VMEM)
    rows, width = cot.shape
    frames = qkv.shape[0]
    columns = qkv.shape[1] // 3
    wide_a, wide_b = 4 * columns, 2 * hid.shape[1]
    dma = pltpu.SemaphoreType.DMA
    shape = jax.ShapeDtypeStruct
    return pl.pallas_call(
        functools.partial(back_kernel, dp, share),
        out_shape=(
            shape((rows, width), BF16),
            shape((rows, width), F32),
            shape((padded, wide_a), F32),
            shape((padded, wide_b), F32),
            shape((16, width), F32),
        ),
        in_specs=[vmem] * len(args),
        out_specs=(vmem,) * 5,
        scratch_shapes=[
            pltpu.VMEM((rows, width), F32),
            pltpu.VMEM((TENSOR, rows, width), BF16),
            pltpu.VMEM(qkv.shape, BF16),
            pltpu.VMEM((zs, 2, padded, wide_a), BF16),
            pltpu.VMEM((zs, 2, padded, wide_b), BF16),
            pltpu.VMEM((TENSOR, rows, width), BF16),
        ]
        + [pltpu.VMEM((columns // HD, frames, HD), F32)] * 2
        + [pltpu.VMEM((TENSOR, 8, width), F32), pltpu.VMEM((dp, 16, width), F32)]
        + scatter_scratch(rows, width) * 3
        + [dma((3,)), dma((3,))]
        + grad_scratch(zs, padded, wide_b)
        + grad_scratch(zs, padded, wide_a)
        + [dma((3,)), dma((3,)), dma((dp,)), dma((dp,))],
        compiler_params=pltpu.CompilerParams(
            collective_id=2, has_side_effects=True, vmem_limit_bytes=VMEM_LIMIT
        ),
    )(*args)


def pad_rows(array, rows, axis):
    extra = rows - array.shape[axis]
    if extra == 0:
        return array
    widths = [(0, 0)] * array.ndim
    widths[axis] = (0, extra)
    return jnp.pad(array, widths)


def body(dp, inputs, cotangent, qkv_weight, proj_weight, up_weight, down_weight, qv_bias, up_bias, norm_gains, row_biases):
    zs = dp // 2
    rows, width = inputs.shape
    share = qkv_weight.shape[1]
    padded = -(-share // 16) * 16
    columns = qkv_weight.shape[2]
    hidden_width = up_weight.shape[1]
    heads = columns // HD
    frames = rows * TENSOR

    def wide(array):
        array = array.reshape(array.shape[0], -1)
        return jnp.pad(array, ((0, 0), (0, 128 - array.shape[1])))

    wa = jnp.concatenate([qkv_weight[0], qkv_weight[1], qkv_weight[2], proj_weight.T], axis=1)
    wb = jnp.concatenate([up_weight, down_weight.T], axis=1)
    bit = norm_gains.shape[1]
    small = jnp.concatenate(
        [wide(norm_gains), wide(row_biases), wide(qv_bias), wide(up_bias[None])], axis=0
    )
    small = pad_rows(small, 16, 0)
    x_all, wa_all, small_all = gather_all(dp, inputs, pad_rows(wa, padded, 0), small)

    def whole(array):
        return array[:, :, :share].reshape(width, array.shape[3])

    x_all = x_all.reshape(frames, width)
    wa_all = whole(wa_all)
    qkv_full, proj_t = wa_all[:, : 3 * columns], wa_all[:, 3 * columns :]
    small_all = small_all.astype(F32)
    tensor = lax.axis_index("tensor")
    vec = small_all[:, :, 0:8, :bit].transpose(2, 0, 1, 3).reshape(8, width)
    mine = lax.dynamic_index_in_dim(small_all, tensor, 1, keepdims=False)
    bits = qv_bias.shape[1]
    qv_full = mine[:, 6:8, :bits].transpose(1, 0, 2).reshape(2, columns)
    up_bias_full = mine[:, 8, : up_bias.shape[0]].reshape(hidden_width)

    normed = layer_norm(x_all.astype(F32), vec[0:1], vec[2:3]).astype(BF16)
    bias_row = jnp.concatenate([qv_full[0], jnp.zeros_like(qv_full[0]), qv_full[1]])
    projected = (jnp.dot(normed, qkv_full, preferred_element_type=F32) + bias_row).astype(BF16)

    def blocks(array):
        return array.reshape(TENSOR, rows, width)

    middle, normed_two, attended, logsum, cot_all, wb_all = make_middle(
        dp, projected, proj_t, inputs, vec, cotangent, pad_rows(wb, padded, 0)
    )
    normed_two = normed_two.reshape(frames, width)
    cot_all = cot_all.reshape(frames, width)
    wb_all = whole(wb_all)
    up_full, down_t = wb_all[:, :hidden_width], wb_all[:, hidden_width:]
    hidden = jnp.dot(normed_two, up_full, preferred_element_type=F32) + up_bias_full
    cumulative = 0.5 * (1.0 + jax.scipy.special.erf(hidden * ROOT_HALF))
    activated = (hidden * cumulative).astype(BF16)
    slope = cumulative + hidden * jnp.exp(-0.5 * hidden * hidden) * ROOT_TWO_PI_INVERSE
    act_grad = jnp.dot(cot_all, down_t, preferred_element_type=F32)
    hidden_grad = (act_grad * slope).astype(BF16)
    grad_part = lax.dot_general(hidden_grad, up_full, LAST, preferred_element_type=F32)
    feed_part = lax.dot_general(activated, down_t, LAST, preferred_element_type=F32)
    up_bias_grad = jnp.sum(hidden_grad.astype(F32), axis=0, keepdims=True)
    outputs, input_grad, ga_out, gb_out, all_sums = go_back(
        dp, share, padded,
        blocks(grad_part.astype(BF16)), blocks(feed_part.astype(BF16)), middle, inputs, cotangent, vec,
        projected, wa_all, logsum, blocks(normed_two), hidden_grad, activated, blocks(cot_all), normed,
        attended, up_bias_grad,
    )
    ga_out, gb_out = ga_out[:share], gb_out[:share]
    place = lax.axis_index("dp")
    both = place * TENSOR + tensor
    qkv_grad_out = ga_out[:, : 3 * columns].reshape(share, 3, columns).transpose(1, 0, 2)
    vectors = lax.dynamic_slice(all_sums, (0, both * bit), (6, bit))
    qv_out = lax.dynamic_slice(all_sums, (9, place * bits), (2, bits))
    up_bits = up_bias.shape[0]
    up_bias_out = lax.dynamic_slice(all_sums, (8, place * up_bits), (1, up_bits))[0]
    return (
        outputs,
        input_grad,
        qkv_grad_out,
        ga_out[:, 3 * columns :].T,
        gb_out[:, :hidden_width],
        gb_out[:, hidden_width:].T,
        qv_out,
        up_bias_out,
        vectors[0:2],
        vectors[2:6],
    )


def solution(mesh):
    both = ("dp", "tensor")
    placed = (
        P(both, None),
        P(both, None),
        P(None, "dp", "tensor"),
        P("tensor", "dp"),
        P("dp", "tensor"),
        P("tensor", "dp"),
        P(None, ("tensor", "dp")),
        P(("tensor", "dp")),
        P(None, both),
        P(None, both),
    )
    return jax.shard_map(
        functools.partial(body, mesh.shape["dp"]),
        mesh=mesh,
        in_specs=placed,
        out_specs=(
            P(both, None),
            P(both, None),
            P(None, "dp", "tensor"),
            P("tensor", "dp"),
            P("dp", "tensor"),
            P("tensor", "dp"),
            P(None, ("tensor", "dp")),
            P(("tensor", "dp")),
            P(None, both),
            P(None, both),
        ),
        check_vma=False,
    )
```
